32 devices in a mesh: fsdp: 16 (over z, y, x), sp: 2 (over core).
Axes of the slice: x: 2, y: 2, z: 4, core: 2. Of those that a mesh axis runs over, the one named last changes fastest.
Arguments:
- latents: bfloat16 [16, 48, 3072], P('fsdp', 'sp'), may hold values from -6 to 6
- step_noise: bfloat16 [16, 48, 3072], P('fsdp', 'sp'), may hold values from -6 to 6
- base_qkv: bfloat16 [3, 3072, 3072], P(None, 'fsdp', 'sp'), may hold values from -1 to 1
- down_qkv: bfloat16 [3, 3072, 64], P(None, 'fsdp'), may hold values from -0.109375 to 0.109375
- up_query_key_value: bfloat16 [3, 64, 3072], P(None, None, 'sp'), may hold values from -0.625 to 0.625
- base_out: bfloat16 [3072, 3072], P('sp', 'fsdp'), may hold values from -0.109375 to 0.109375
- down_out: bfloat16 [3072, 64], P('sp'), may hold values from -0.109375 to 0.109375
- up_out: bfloat16 [64, 3072], P(None, 'fsdp'), may hold values from -0.625 to 0.625
- modulation: float32 [16, 3, 3072], replicated, may hold values from -3 to 3
- timestep: int32 [16], P('fsdp'), may hold values from 0 to 14
Outputs:
- velocity: bfloat16 [16, 48, 3072], P('fsdp', 'sp')
- next_latents: bfloat16 [16, 48, 3072], P('fsdp', 'sp')
The draws below stay inside these ranges and needn't reach their ends.
Inputs may be any that keep to these rules, and one draw needn't show every extreme that they name: timestep[n] + 1 is also a step of the plan.
All inputs are finite; a program needn't handle non-finite values.
Results may differ from the reference program's by a relative error of at most 0.02.
Values may be sent and summed in bfloat16 or wider, within the bound.
A program may use at most 128 MiB of HBM per device.

```python
import math
import jax
import jax.numpy as jnp
from jax import lax

HEADS = 24
HEAD_DIM = 128
D = 3072
RANK = 64
NSTEP = 16
LEN = 48
SAMPLES = 16
N_SP = 2


def draw_base_qkv(key, part):
    key = jax.random.fold_in(key, 11)
    first = jax.random.fold_in(key, 0)
    columns = HEADS * HEAD_DIM
    stacked = jnp.clip(jax.random.normal(first, (3, D, columns), jnp.float32), -4.0, 4.0) / math.sqrt(D)
    return jnp.clip(stacked, -0.9, 0.9).astype(jnp.bfloat16)


def touch_ends(result, rng, least, high):
    shape = result.shape
    spot = [jax.random.randint(jax.random.fold_in(rng, axis), (), 0, shape[axis]) for axis in range(len(shape))]
    result = result.at[tuple(spot)].set(least)
    longest = shape.index(max(shape))
    spot[longest] = (spot[longest] + 1) % shape[longest]
    return result.at[tuple(spot)].set(high)


def levels(own_key, extent, pieces, least, largest):
    def one(axis_at, parts):
        draws = jax.random.uniform(jax.random.fold_in(jax.random.fold_in(own_key, 6), axis_at), (parts,), jnp.float32, least / len(pieces), largest / len(pieces))
        return jnp.repeat(jnp.exp(draws), extent[axis_at] // parts).reshape((-1,) + (1,) * (len(extent) - axis_at - 1))

    factor_of = one(*pieces[0])
    for cut in pieces[1:]:
        factor_of = factor_of * one(*cut)
    return factor_of


def scatter_about(rng, dims, scale, most, pieces=(), dtype=jnp.bfloat16):
    entries = scale * jax.random.normal(rng, dims, jnp.float32)
    if pieces:
        entries = entries * levels(rng, dims, pieces, -0.22, 0.18)
    return jnp.clip(entries, -most, most).astype(dtype)


def setup_inputs(seed: int = 0) -> dict:
    seeds = jax.random.split(jax.random.key(seed), 11)
    return {
        "latents": scatter_about(seeds[0], (SAMPLES, LEN, D), 1.0, 6.0, ((0, 16), (1, 2))),
        "step_noise": scatter_about(seeds[1], (SAMPLES, LEN, D), 1.0, 6.0, ((0, 16), (1, 2))),
        "base_qkv": draw_base_qkv(jax.random.fold_in(seeds[10], 71), 0),
        "down_qkv": scatter_about(seeds[3], (3, D, RANK), D ** -0.5, 0.109375, ((1, 16),)),
        "up_query_key_value": scatter_about(seeds[4], (3, RANK, HEADS * HEAD_DIM), 0.04, 0.625, ((2, 2),)),
        "base_out": scatter_about(seeds[5], (HEADS * HEAD_DIM, D), (HEADS * HEAD_DIM) ** -0.5, 0.109375, ((0, 2), (1, 16))),
        "down_out": scatter_about(seeds[6], (HEADS * HEAD_DIM, RANK), (HEADS * HEAD_DIM) ** -0.5, 0.109375, ((0, 2),)),
        "up_out": scatter_about(seeds[7], (RANK, D), 0.04, 0.625, ((1, 16),)),
        "modulation": scatter_about(seeds[8], (NSTEP, 3, D), 0.5, 3.0, (), jnp.float32),
        "timestep": touch_ends(jax.random.randint(seeds[9], (SAMPLES,), 0, NSTEP - 1), jax.random.fold_in(seeds[9], 1), 0, (NSTEP - 1) - 1).astype(jnp.int32),
    }


EPSILON = 1e-06
SHIFT_FACTOR = 5.0
NOISE_LEVEL = 0.7

def plan_sigma(position):
    ramp = 1.0 - position / NSTEP
    return SHIFT_FACTOR * ramp / (1.0 + (SHIFT_FACTOR - 1.0) * ramp)

def reference(latents, step_noise, base_qkv, down_qkv, up_query_key_value, base_out, down_out, up_out, modulation, timestep):
    merged_qkv = (base_qkv.astype(jnp.float32) + jnp.einsum('pdr,prc->pdc', down_qkv.astype(jnp.float32), up_query_key_value.astype(jnp.float32))).astype(jnp.bfloat16)
    merged_out = (base_out.astype(jnp.float32) + jnp.dot(down_out, up_out, preferred_element_type=jnp.float32)).astype(jnp.bfloat16)
    group_cols = HEADS * HEAD_DIM // N_SP
    grouped_output = merged_out.astype(jnp.float32).reshape(N_SP, group_cols, D)

    def one_sample(packed):
        latent, noise_rows, step_index = packed
        mod_rows = lax.dynamic_index_in_dim(modulation, step_index, 0, keepdims=False)
        latent_f = latent.astype(jnp.float32)
        mean_square = lax.optimization_barrier(jnp.mean(latent_f * latent_f, axis=-1, keepdims=True))
        normalized_rows = (latent_f * lax.rsqrt(mean_square + EPSILON) * (1.0 + mod_rows[1]) + mod_rows[0]).astype(jnp.bfloat16)
        projected = jnp.einsum('ld,pdc->plc', normalized_rows.astype(jnp.float32), merged_qkv.astype(jnp.float32)).astype(jnp.bfloat16)
        split_heads = projected.reshape(3, LEN, HEADS, HEAD_DIM).transpose(0, 2, 1, 3).astype(jnp.float32)
        scores = jnp.einsum('hqe,hke->hqk', split_heads[0], split_heads[1]) * (1.0 / HEAD_DIM ** 0.5)
        attention_weights = jax.nn.softmax(scores, axis=-1).astype(jnp.bfloat16)
        attention_result = jnp.einsum('hqk,hke->hqe', attention_weights.astype(jnp.float32), split_heads[2]).astype(jnp.bfloat16)
        attention_result = attention_result.transpose(1, 0, 2).reshape(LEN, N_SP, group_cols).astype(jnp.float32)
        partial_sums = jnp.einsum('tmy,mya->mta', attention_result, grouped_output).astype(jnp.bfloat16)
        block_out = lax.optimization_barrier(jnp.sum(partial_sums.astype(jnp.float32), axis=0))
        velocity = ((1.0 + mod_rows[2]) * block_out).astype(jnp.bfloat16)
        position = step_index.astype(jnp.float32)
        step_size = plan_sigma(position + 1.0) - plan_sigma(position)
        next_rows = latent_f + step_size * velocity.astype(jnp.float32) + NOISE_LEVEL * jnp.sqrt(-step_size) * noise_rows.astype(jnp.float32)
        return (velocity, next_rows.astype(jnp.bfloat16))
    velocity, next_latents = lax.map(one_sample, (latents, step_noise, timestep))
    return (velocity, next_latents)
```

```python
import functools

import jax
import jax.numpy as jnp
from jax import lax
from jax.experimental import pallas as pl
from jax.experimental.pallas import tpu as pltpu
from jax.sharding import PartitionSpec as P

HEAD_DIM = 128
NSTEP = 16


EPSILON = 1e-06
SHIFT_FACTOR = 5.0
NOISE_LEVEL = 0.7


def plan_sigma(position):
    ramp = 1.0 - position / NSTEP
    return SHIFT_FACTOR * ramp / (1.0 + (SHIFT_FACTOR - 1.0) * ramp)


PLANE = 4
MESH = pl.DeviceIdType.MESH


def plane_kernel(
    n_z,
    step_ref,
    latents_ref,
    noise_ref,
    base_qkv_ref,
    down_qkv_ref,
    up_qkv_ref,
    base_out_ref,
    down_out_ref,
    up_out_ref,
    mod_ref,
    velocity_ref,
    next_ref,
    latf,
    normed,
    acts,
    w_send,
    w_recv,
    part_send,
    part_recv,
    part_own,
    att_send,
    att_all,
    wo_all,
    out_half,
    out_sib,
    vel_send,
    vel_recv,
    lat_sem,
    x1_sem,
    x3_sem,
    xs_sem,
    w_sem,
    p_sem,
    wo_sem,
    at_sem,
    ag_sem,
    os_sem,
    v_sem,
):
    f, c = lax.axis_index("fsdp"), lax.axis_index("sp")
    z, j = f // PLANE, f % PLANE
    rows, d_model = latents_ref.shape
    tokens = 2 * rows
    n_head = w_send.shape[0]
    block = d_model // n_z
    half = block // 2
    w_rows = base_qkv_ref.shape[1]
    width = 3 * HEAD_DIM
    f32, bf16 = jnp.float32, jnp.bfloat16

    def in_plane(d):
        return (z * PLANE + (j + d) % PLANE, c)

    def in_column(d):
        return (((z + d) % n_z) * PLANE + j, c)

    sibling = (f, 1 - c)

    def send(src, dst, sems, where, device):
        copy = pltpu.make_async_remote_copy(
            src_ref=src,
            dst_ref=dst,
            send_sem=sems.at[(0, *where)],
            recv_sem=sems.at[(1, *where)],
            device_id=device,
            device_id_type=MESH,
        )
        copy.start()
        return copy

    started = []
    barrier = pltpu.get_barrier_semaphore()
    partners = [sibling]
    partners += [in_plane(d) for d in range(1, PLANE)]
    partners += [in_column(d) for d in range(1, n_z)]
    for partner in partners:
        pl.semaphore_signal(barrier, inc=1, device_id=partner, device_id_type=MESH)

    latf[c] = latents_ref[...].astype(f32)
    for p in range(3):
        merged = (
            base_qkv_ref[p].astype(f32)
            + jnp.dot(down_qkv_ref[p], up_qkv_ref[p], preferred_element_type=f32)
        ).astype(bf16)
        for g in range(PLANE):
            for h in range(n_head):
                at = (g * n_head + h) * HEAD_DIM
                w_send[h, g, :, p * HEAD_DIM : (p + 1) * HEAD_DIM] = merged[:, at : at + HEAD_DIM]
    pl.semaphore_wait(barrier, len(partners))

    lat_copy = send(latf.at[c], latf.at[c], lat_sem, (), sibling)
    w_copies = {}

    def send_weights(h):
        for d in range(1, PLANE):
            w_copies[h, d] = send(
                w_send.at[h, (j + d) % PLANE], w_recv.at[h, j], w_sem, (h, d - 1), in_plane(d)
            )

    send_weights(0)
    for h in range(n_head):
        w_recv[h, j] = w_send[h, j]

    step_index = step_ref[0]
    mod_rows = mod_ref[step_index]
    lat_copy.wait_recv()
    lat_rows = latf[...].reshape(tokens, d_model)
    mean_square = jnp.mean(lat_rows * lat_rows, axis=-1, keepdims=True)
    normed[...] = (
        lat_rows * lax.rsqrt(mean_square + EPSILON) * (1.0 + mod_rows[1:2]) + mod_rows[0:1]
    ).astype(bf16)

    def features(z_at):
        return pl.ds(pl.multiple_of(z_at * block + c * half, half), half)

    x1 = [
        send(
            normed.at[:, features((z + d) % n_z)],
            acts.at[c, z, j],
            x1_sem,
            (d - 1,),
            in_column(d),
        )
        for d in range(1, n_z)
    ]
    acts[c, z, j] = normed[:, features(z)]
    for copy in x1:
        copy.wait_recv()
    x3 = [
        send(acts.at[c, :, j], acts.at[c, :, j], x3_sem, (d - 1,), in_plane(d))
        for d in range(1, PLANE)
    ]
    xs = [send(acts.at[c, :, j], acts.at[c, :, j], xs_sem, (0,), sibling)]
    for h in range(1, n_head):
        send_weights(h)
    merged_out = (
        base_out_ref[...].astype(f32).T
        + lax.dot_general(
            up_out_ref[...],
            down_out_ref[...],
            (((0,), (1,)), ((), ())),
            preferred_element_type=f32,
        )
    ).astype(bf16)
    for g in range(PLANE):
        for h in range(n_head):
            at, to = (g * n_head + h) * HEAD_DIM, (h * PLANE + g) * HEAD_DIM
            wo_all[j, :, to : to + HEAD_DIM] = merged_out[:, at : at + HEAD_DIM]
    for d in range(1, PLANE):
        x3[d - 1].wait_recv()
        came = (j + PLANE - d) % PLANE
        xs.append(send(acts.at[c, :, came], acts.at[c, :, came], xs_sem, (d,), sibling))
    wo = [
        send(wo_all.at[j], wo_all.at[j], wo_sem, (d - 1,), in_plane(d)) for d in range(1, PLANE)
    ]
    for copy in xs:
        copy.wait_recv()

    p_copies = {}
    for h in range(n_head):
        for d in range(1, PLANE):
            w_copies[h, d].wait_recv()
        weights = w_recv[h].reshape(PLANE * w_rows, width)
        for d in list(range(1, n_z)) + [0]:
            z_at = (z + d) % n_z
            part = jnp.dot(
                acts[0, z_at].reshape(PLANE * tokens, half),
                weights[:half],
                preferred_element_type=f32,
            ) + jnp.dot(
                acts[1, z_at].reshape(PLANE * tokens, half),
                weights[half:],
                preferred_element_type=f32,
            )
            if d:
                part_send[h, z_at] = part.astype(bf16)
                p_copies[h, d] = send(
                    part_send.at[h, z_at], part_recv.at[h, d - 1], p_sem, (h, d - 1), in_column(d)
                )
            else:
                part_own[h] = part

    at_copies, ag_copies = {}, {}

    def lanes(h, g):
        return pl.ds(pl.multiple_of((h * PLANE + g) * HEAD_DIM, HEAD_DIM), HEAD_DIM)

    def spread(h):
        for d in range(1, PLANE):
            at_copies[h, d].wait_recv()
        chunk = pl.ds(h * PLANE * HEAD_DIM, PLANE * HEAD_DIM)
        for d in range(1, n_z):
            ag_copies[h, d] = send(
                att_all.at[z, :, chunk],
                att_all.at[z, :, chunk],
                ag_sem,
                (h, d - 1),
                in_column(d),
            )

    for h in range(n_head):
        total = part_own[h]
        for d in range(1, n_z):
            p_copies[h, d].wait_recv()
            total = total + part_recv[h, d - 1].astype(f32)
        projected = total.astype(bf16)
        for s in range(PLANE):
            rows_s = projected[s * tokens : (s + 1) * tokens]
            query = rows_s[:, :HEAD_DIM]
            key = rows_s[:, HEAD_DIM : 2 * HEAD_DIM]
            value = rows_s[:, 2 * HEAD_DIM :]
            scores = lax.dot_general(
                query, key, (((1,), (1,)), ((), ())), preferred_element_type=f32
            ) * (1.0 / HEAD_DIM**0.5)
            weights = jnp.exp(scores - jnp.max(scores, axis=-1, keepdims=True))
            weights = weights / jnp.sum(weights, axis=-1, keepdims=True)
            att_send[h, s] = jnp.dot(
                weights.astype(bf16), value, preferred_element_type=f32
            ).astype(bf16)
        for d in range(1, PLANE):
            at_copies[h, d] = send(
                att_send.at[h, (j + d) % PLANE],
                att_all.at[z, :, lanes(h, j)],
                at_sem,
                (h, d - 1),
                in_plane(d),
            )
        att_all[z, :, lanes(h, j)] = att_send[h, j]
        if h:
            spread(h - 1)
    spread(n_head - 1)

    for copy in wo:
        copy.wait_recv()
    for copy in ag_copies.values():
        copy.wait_recv()
    out = lax.dot_general(
        att_all[...].reshape(n_z * tokens, att_all.shape[2]),
        wo_all[...].reshape(block, att_all.shape[2]),
        (((1,), (1,)), ((), ())),
        preferred_element_type=f32,
    )
    for s in range(n_z):
        for k in range(2):
            at = s * tokens + k * rows
            out_half[k, s] = out[at : at + rows]
    os_copy = send(out_half.at[1 - c], out_sib, os_sem, (), sibling)
    os_copy.wait_recv()
    pad = jnp.zeros((vel_send.shape[1] - rows, block), f32)
    v_copies = []
    for d in list(range(1, n_z)) + [0]:
        z_at = (z + d) % n_z
        block_sum = out_half[c, z_at] + out_sib[z_at]
        block_sum = jnp.concatenate([block_sum, pad], axis=0).astype(bf16)
        if d:
            vel_send[z_at] = block_sum
            v_copies.append(
                send(vel_send.at[z_at], vel_recv.at[z], v_sem, (d - 1,), in_column(d))
            )
        else:
            vel_recv[z] = block_sum

    position = jnp.full((1, block), step_index.astype(f32), f32)
    step_size = plan_sigma(position + 1.0) - plan_sigma(position)
    noise_size = NOISE_LEVEL * jnp.sqrt(-step_size)
    for copy in v_copies:
        copy.wait_recv()
    for s in range(n_z):
        cols = slice(s * block, (s + 1) * block)
        block_out = vel_recv[s].astype(f32)[:rows]
        velocity = ((1.0 + mod_rows[2:3, cols]) * block_out).astype(bf16)
        velocity_ref[:, cols] = velocity
        next_ref[:, cols] = (
            latf[c, :, cols]
            + step_size * velocity.astype(f32)
            + noise_size * noise_ref[:, cols].astype(f32)
        ).astype(bf16)

    every = [lat_copy, os_copy, *x1, *x3, *xs, *wo, *v_copies]
    for group in (w_copies, p_copies, at_copies, ag_copies):
        every += list(group.values())
    for copy in every:
        copy.wait_send()


def per_device(*args):
    latents, step_noise, base_qkv, down_qkv, up_qkv, base_out, down_out, up_out, modulation, step = (
        args
    )
    n_fsdp, n_sp = lax.axis_size("fsdp"), lax.axis_size("sp")
    _, rows, d_model = latents.shape
    heads_here = base_qkv.shape[2] // HEAD_DIM
    tokens = rows * n_sp
    if n_sp != 2 or n_fsdp % PLANE or heads_here % PLANE or tokens % 16:
        return gather_weights(*args)
    n_z, n_head = n_fsdp // PLANE, heads_here // PLANE
    block = d_model // n_z
    half = block // 2
    w_rows = base_qkv.shape[1]
    width = 3 * HEAD_DIM
    cols = base_qkv.shape[2]
    f32, bf16 = jnp.float32, jnp.bfloat16
    if half % HEAD_DIM or w_rows % 16 or block != PLANE * w_rows or base_out.shape[1] != w_rows:
        return gather_weights(*args)
    padded = -(-rows // 16) * 16
    dma = pltpu.SemaphoreType.DMA
    vmem = pl.BlockSpec(memory_space=pltpu.VMEM)
    velocity, next_rows = pl.pallas_call(
        functools.partial(plane_kernel, n_z),
        out_shape=[jax.ShapeDtypeStruct((rows, d_model), bf16)] * 2,
        in_specs=[pl.BlockSpec(memory_space=pltpu.SMEM)] + [vmem] * 9,
        out_specs=[vmem] * 2,
        scratch_shapes=[
            pltpu.VMEM((2, rows, d_model), f32),
            pltpu.VMEM((tokens, d_model), bf16),
            pltpu.VMEM((2, n_z, PLANE, tokens, half), bf16),
            pltpu.VMEM((n_head, PLANE, w_rows, width), bf16),
            pltpu.VMEM((n_head, PLANE, w_rows, width), bf16),
            pltpu.VMEM((n_head, n_z, PLANE * tokens, width), bf16),
            pltpu.VMEM((n_head, n_z - 1, PLANE * tokens, width), bf16),
            pltpu.VMEM((n_head, PLANE * tokens, width), f32),
            pltpu.VMEM((n_head, PLANE, tokens, HEAD_DIM), bf16),
            pltpu.VMEM((n_z, tokens, cols), bf16),
            pltpu.VMEM((PLANE, w_rows, cols), bf16),
            pltpu.VMEM((2, n_z, rows, block), f32),
            pltpu.VMEM((n_z, rows, block), f32),
            pltpu.VMEM((n_z, padded, block), bf16),
            pltpu.VMEM((n_z, padded, block), bf16),
            dma((2,)),
            dma((2, n_z - 1)),
            dma((2, PLANE - 1)),
            dma((2, PLANE)),
            dma((2, n_head, PLANE - 1)),
            dma((2, n_head, n_z - 1)),
            dma((2, PLANE - 1)),
            dma((2, n_head, PLANE - 1)),
            dma((2, n_head, n_z - 1)),
            dma((2,)),
            dma((2, n_z - 1)),
        ],
        compiler_params=pltpu.CompilerParams(
            collective_id=0, has_side_effects=True, vmem_limit_bytes=48 * 1024 * 1024
        ),
        cost_estimate=pl.CostEstimate(
            flops=2 * n_fsdp * tokens * w_rows * 4 * cols,
            bytes_accessed=8 * w_rows * cols,
            transcendentals=0,
        ),
    )(
        step,
        latents[0],
        step_noise[0],
        base_qkv,
        down_qkv,
        up_qkv,
        base_out,
        down_out,
        up_out,
        modulation,
    )
    return (velocity[None], next_rows[None])


def gather_weights(
    latents,
    step_noise,
    base_qkv,
    down_qkv,
    up_query_key_value,
    base_out,
    down_out,
    up_out,
    modulation,
    timestep,
):
    step_index = timestep[0]
    mod_rows = lax.dynamic_index_in_dim(modulation, step_index, 0, keepdims=False)
    latent_f = latents[0].astype(jnp.float32)
    mean_square = jnp.mean(latent_f * latent_f, axis=-1, keepdims=True)
    normalized_rows = (
        latent_f * lax.rsqrt(mean_square + EPSILON) * (1.0 + mod_rows[1]) + mod_rows[0]
    ).astype(jnp.bfloat16)
    head_cols = base_qkv.shape[2]
    seq_len = normalized_rows.shape[0] * lax.axis_size("sp")
    every_token = lax.all_gather(normalized_rows, "sp", axis=0, tiled=True)
    lowrank = jnp.einsum(
        "prk,pkc->prc", down_qkv, up_query_key_value, preferred_element_type=jnp.float32
    )
    merged_qkv = (base_qkv.astype(jnp.float32) + lowrank).astype(jnp.bfloat16)
    projected = jnp.einsum(
        "lr,prc->plc",
        every_token,
        lax.all_gather(merged_qkv, "fsdp", axis=1, tiled=True),
        preferred_element_type=jnp.float32,
    ).astype(jnp.bfloat16)
    heads_here = head_cols // HEAD_DIM
    split_heads = projected.reshape(3, seq_len, heads_here, HEAD_DIM).transpose(2, 0, 1, 3)

    def one_head(triple):
        scores = jnp.dot(triple[0], triple[1].T, preferred_element_type=jnp.float32) * (
            1.0 / HEAD_DIM**0.5
        )
        attention_weights = jax.nn.softmax(scores, axis=-1).astype(jnp.bfloat16)
        return jnp.dot(attention_weights, triple[2], preferred_element_type=jnp.float32).astype(
            jnp.bfloat16
        )

    per_head = lax.map(one_head, split_heads)
    attention_result = per_head.transpose(1, 0, 2).reshape(seq_len, head_cols)
    merged_out = (
        base_out.astype(jnp.float32) + jnp.dot(down_out, up_out, preferred_element_type=jnp.float32)
    ).astype(jnp.bfloat16)
    full_out = lax.all_gather(merged_out, "fsdp", axis=1, tiled=True)
    block_out = lax.psum_scatter(
        jnp.dot(attention_result, full_out, preferred_element_type=jnp.float32).astype(
            jnp.bfloat16
        ),
        "sp",
        scatter_dimension=0,
        tiled=True,
    ).astype(jnp.float32)
    velocity = ((1.0 + mod_rows[2]) * block_out).astype(jnp.bfloat16)
    position = step_index.astype(jnp.float32)
    step_size = plan_sigma(position + 1.0) - plan_sigma(position)
    next_rows = (
        latent_f
        + step_size * velocity.astype(jnp.float32)
        + NOISE_LEVEL * jnp.sqrt(-step_size) * step_noise[0].astype(jnp.float32)
    )
    return (velocity[None], next_rows.astype(jnp.bfloat16)[None])


def solution(mesh):
    in_specs = (
        P("fsdp", "sp", None),
        P("fsdp", "sp", None),
        P(None, "fsdp", "sp"),
        P(None, "fsdp", None),
        P(None, None, "sp"),
        P("sp", "fsdp"),
        P("sp", None),
        P(None, "fsdp"),
        P(),
        P("fsdp"),
    )
    out_specs = (P("fsdp", "sp", None), P("fsdp", "sp", None))
    return jax.shard_map(
        per_device, mesh=mesh, in_specs=in_specs, out_specs=out_specs, check_vma=False
    )
```

```python
import functools

import jax
import jax.numpy as jnp
from jax import lax
from jax.experimental import pallas as pl
from jax.experimental.pallas import tpu as pltpu
from jax.sharding import PartitionSpec as P

HEAD_DIM = 128
NSTEP = 16


EPSILON = 1e-06
SHIFT_FACTOR = 5.0
NOISE_LEVEL = 0.7


def plan_sigma(position):
    ramp = 1.0 - position / NSTEP
    return SHIFT_FACTOR * ramp / (1.0 + (SHIFT_FACTOR - 1.0) * ramp)


PLANE = 4
MESH = pl.DeviceIdType.MESH


def plane_kernel(
    n_z,
    step_ref,
    latents_ref,
    noise_ref,
    base_qkv_ref,
    down_qkv_ref,
    up_qkv_ref,
    base_out_ref,
    down_out_ref,
    up_out_ref,
    mod_ref,
    velocity_ref,
    next_ref,
    latf,
    normed,
    acts,
    w_send,
    w_recv,
    part_send,
    part_recv,
    part_own,
    att_send,
    att_all,
    wo_all,
    out_half,
    out_sib,
    vel_send,
    vel_recv,
    lat_sem,
    x1_sem,
    x3_sem,
    xs_sem,
    w_sem,
    pair_sem,
    far_sem,
    wo_sem,
    at_sem,
    ag_sem,
    os_sem,
    v_sem,
):
    f, c = lax.axis_index("fsdp"), lax.axis_index("sp")
    z, j = f // PLANE, f % PLANE
    rows, d_model = latents_ref.shape
    tokens = 2 * rows
    n_head = w_send.shape[0]
    block = d_model // n_z
    half = block // 2
    w_rows = base_qkv_ref.shape[1]
    x_at, y_at = j % 2, j // 2
    z_lo, z_hi = z % 2, z // 2
    x_near, y_near = 2 * y_at + 1 - x_at, 2 * (1 - y_at) + x_at
    width = 3 * HEAD_DIM
    f32, bf16 = jnp.float32, jnp.bfloat16

    def in_plane(d):
        return (z * PLANE + (j + d) % PLANE, c)

    def in_column(d):
        return (((z + d) % n_z) * PLANE + j, c)

    sibling = (f, 1 - c)
    x_device, y_device = (z * PLANE + x_near, c), (z * PLANE + y_near, c)
    z_pair = ((2 * z_hi + 1 - z_lo) * PLANE + j, c)
    z_far = ((2 * (1 - z_hi) + z_lo) * PLANE + j, c)

    def send(src, dst, sems, where, device):
        copy = pltpu.make_async_remote_copy(
            src_ref=src,
            dst_ref=dst,
            send_sem=sems.at[(0, *where)],
            recv_sem=sems.at[(1, *where)],
            device_id=device,
            device_id_type=MESH,
        )
        copy.start()
        return copy

    barrier = pltpu.get_barrier_semaphore()
    partners = [sibling]
    partners += [in_plane(d) for d in range(1, PLANE)]
    partners += [in_column(d) for d in range(1, n_z)]
    for partner in partners:
        pl.semaphore_signal(barrier, inc=1, device_id=partner, device_id_type=MESH)

    latf[c] = latents_ref[...].astype(f32)

    def merge(h):
        for g in range(PLANE):
            at = (g * n_head + h) * HEAD_DIM
            for p in range(3):
                lowrank = lax.dot_general(
                    down_qkv_ref[p],
                    up_qkv_ref[p, :, at : at + HEAD_DIM],
                    (((0,), (0,)), ((), ())),
                    preferred_element_type=f32,
                )
                w_send[h, g, :, p * HEAD_DIM : (p + 1) * HEAD_DIM] = (
                    base_qkv_ref[p, :, at : at + HEAD_DIM].astype(f32) + lowrank
                ).astype(bf16)
        w_recv[h, j] = w_send[h, j]

    pl.semaphore_wait(barrier, len(partners))
    lat_copy = send(latf.at[c], latf.at[c], lat_sem, (), sibling)
    w_copies = {}

    def send_weights(h):
        for d in range(1, PLANE):
            w_copies[h, d] = send(
                w_send.at[h, (j + d) % PLANE], w_recv.at[h, j], w_sem, (h, d - 1), in_plane(d)
            )

    merge(0)
    send_weights(0)

    step_index = step_ref[0]

    def mod_row(k):
        return mod_ref[k, pl.ds(step_index, 1), :]

    lat_copy.wait_recv()
    lat_rows = latf[...].reshape(tokens, d_model)
    mean_square = jnp.mean(lat_rows * lat_rows, axis=-1, keepdims=True)
    normed[...] = (
        lat_rows * lax.rsqrt(mean_square + EPSILON) * (1.0 + mod_row(1)) + mod_row(0)
    ).astype(bf16)

    def features(z_at):
        return pl.ds(pl.multiple_of(z_at * block + c * half, half), half)

    x1 = [
        send(
            normed.at[:, features((z + d) % n_z)],
            acts.at[c, z, j],
            x1_sem,
            (d - 1,),
            in_column(d),
        )
        for d in range(1, n_z)
    ]
    acts[c, z, j] = normed[:, features(z)]
    if n_head > 1:
        merge(1)
    for copy in x1:
        copy.wait_recv()
    x3 = [
        send(acts.at[c, :, j], acts.at[c, :, j], x3_sem, (d - 1,), in_plane(d))
        for d in range(1, PLANE)
    ]
    xs = [send(acts.at[c, :, j], acts.at[c, :, j], xs_sem, (0,), sibling)]
    for h in range(1, n_head):
        if h > 1:
            merge(h)
        send_weights(h)
    merged_out = (
        base_out_ref[...].astype(f32)
        + lax.dot_general(
            up_out_ref[...],
            down_out_ref[...],
            (((0,), (0,)), ((), ())),
            preferred_element_type=f32,
        )
    ).astype(bf16)
    for g in range(PLANE):
        for h in range(n_head):
            at, to = (g * n_head + h) * HEAD_DIM, (h * PLANE + g) * HEAD_DIM
            wo_all[j, :, to : to + HEAD_DIM] = merged_out[:, at : at + HEAD_DIM]
    for d in range(1, PLANE):
        x3[d - 1].wait_recv()
        came = (j + PLANE - d) % PLANE
        xs.append(send(acts.at[c, :, came], acts.at[c, :, came], xs_sem, (d,), sibling))
    for copy in xs:
        copy.wait_recv()

    wo_x, wo_y, wo_far = [], [], []
    wo_half = w_rows // 2

    def send_out_rows(owner, k, where, device):
        view = wo_all.at[owner, pl.ds(k * wo_half, wo_half)]
        return send(view, view, wo_sem, where, device)

    pair_copies, far_copies = {}, {}
    for h in range(n_head):
        for d in range(1, PLANE):
            w_copies[h, d].wait_recv()
        weights = w_recv[h].reshape(PLANE * w_rows, width)
        for parity, hi in ((1, 1), (1, 0), (0, 1), (0, 0)):
            z_at = 2 * ((z_hi + hi) % 2) + (z_lo + parity) % 2
            part = jnp.dot(
                acts[0, z_at].reshape(PLANE * tokens, half),
                weights[:half],
                preferred_element_type=f32,
            ) + jnp.dot(
                acts[1, z_at].reshape(PLANE * tokens, half),
                weights[half:],
                preferred_element_type=f32,
            )
            if parity:
                part_send[h, hi] = part.astype(bf16)
                pair_copies[h, hi] = send(
                    part_send.at[h, hi], part_recv.at[h, hi], pair_sem, (h, hi), z_pair
                )
            else:
                part_own[h, hi] = part
        if h == min(1, n_head - 1):
            for k in range(2):
                wo_x.append(send_out_rows(j, k, (0, k), x_device))
                wo_y.append(send_out_rows(j, 1 - k, (1, 1 - k), y_device))

    def send_far(h):
        pair_copies[h, 1].wait_recv()
        part_send[h, 2] = (part_own[h, 1] + part_recv[h, 1].astype(f32)).astype(bf16)
        far_copies[h] = send(part_send.at[h, 2], part_recv.at[h, 2], far_sem, (h,), z_far)

    at_copies, ag_copies = {}, {}

    def lanes(h, g):
        return pl.ds(pl.multiple_of((h * PLANE + g) * HEAD_DIM, HEAD_DIM), HEAD_DIM)

    def spread(h):
        for d in range(1, PLANE):
            at_copies[h, d].wait_recv()
        chunk = pl.ds(h * PLANE * HEAD_DIM, PLANE * HEAD_DIM)
        for d in range(1, n_z):
            ag_copies[h, d] = send(
                att_all.at[z, :, chunk],
                att_all.at[z, :, chunk],
                ag_sem,
                (h, d - 1),
                in_column(d),
            )

    def attend(h):
        pair_copies[h, 0].wait_recv()
        far_copies[h].wait_recv()
        projected = (
            part_own[h, 0] + part_recv[h, 0].astype(f32) + part_recv[h, 2].astype(f32)
        ).astype(bf16)
        for s in range(PLANE):
            rows_s = projected[s * tokens : (s + 1) * tokens]
            query = rows_s[:, :HEAD_DIM]
            key = rows_s[:, HEAD_DIM : 2 * HEAD_DIM]
            value = rows_s[:, 2 * HEAD_DIM :]
            scores = lax.dot_general(
                query, key, (((1,), (1,)), ((), ())), preferred_element_type=f32
            ) * (1.0 / HEAD_DIM**0.5)
            weights = jnp.exp(scores - jnp.max(scores, axis=-1, keepdims=True))
            weights = weights / jnp.sum(weights, axis=-1, keepdims=True)
            att_send[h, s] = jnp.dot(
                weights.astype(bf16), value, preferred_element_type=f32
            ).astype(bf16)
        for d in range(1, PLANE):
            at_copies[h, d] = send(
                att_send.at[h, (j + d) % PLANE],
                att_all.at[z, :, lanes(h, j)],
                at_sem,
                (h, d - 1),
                in_plane(d),
            )
        att_all[z, :, lanes(h, j)] = att_send[h, j]

    send_far(0)
    for h in range(n_head):
        if h + 1 < n_head:
            send_far(h + 1)
        else:
            wo_x[0].wait_recv()
            wo_far.append(send_out_rows(x_near, 0, (2, 0), y_device))
            wo_y[0].wait_recv()
            wo_far.append(send_out_rows(y_near, 1, (2, 1), x_device))
        attend(h)
        if h:
            spread(h - 1)
    spread(n_head - 1)

    for copy in (wo_x[1], wo_y[1], *wo_far):
        copy.wait_recv()
    out = None
    for h in range(n_head):
        for d in range(1, n_z):
            ag_copies[h, d].wait_recv()
        chunk = slice(h * PLANE * HEAD_DIM, (h + 1) * PLANE * HEAD_DIM)
        term = lax.dot_general(
            att_all[:, :, chunk].reshape(n_z * tokens, PLANE * HEAD_DIM),
            wo_all[:, :, chunk].reshape(block, PLANE * HEAD_DIM),
            (((1,), (1,)), ((), ())),
            preferred_element_type=f32,
        )
        out = term if out is None else out + term
    for s in range(n_z):
        for k in range(2):
            at = s * tokens + k * rows
            out_half[k, s] = out[at : at + rows]
    os_copy = send(out_half.at[1 - c], out_sib, os_sem, (), sibling)
    os_copy.wait_recv()
    pad = jnp.zeros((vel_send.shape[1] - rows, block), f32)
    v_copies = []
    for d in list(range(1, n_z)) + [0]:
        z_at = (z + d) % n_z
        block_sum = out_half[c, z_at] + out_sib[z_at]
        block_sum = jnp.concatenate([block_sum, pad], axis=0).astype(bf16)
        if d:
            vel_send[z_at] = block_sum
            v_copies.append(
                send(vel_send.at[z_at], vel_recv.at[z], v_sem, (d - 1,), in_column(d))
            )
        else:
            vel_recv[z] = block_sum

    gate = mod_row(2)
    position = jnp.full((1, block), step_index.astype(f32), f32)
    step_size = plan_sigma(position + 1.0) - plan_sigma(position)
    noise_size = NOISE_LEVEL * jnp.sqrt(-step_size)
    for copy in v_copies:
        copy.wait_recv()
    for s in range(n_z):
        cols = slice(s * block, (s + 1) * block)
        block_out = vel_recv[s].astype(f32)[:rows]
        velocity = ((1.0 + gate[:, cols]) * block_out).astype(bf16)
        velocity_ref[:, cols] = velocity
        next_ref[:, cols] = (
            latf[c, :, cols]
            + step_size * velocity.astype(f32)
            + noise_size * noise_ref[:, cols].astype(f32)
        ).astype(bf16)

    every = [lat_copy, os_copy, *x1, *x3, *xs, *wo_x, *wo_y, *wo_far, *v_copies]
    for group in (w_copies, pair_copies, far_copies, at_copies, ag_copies):
        every += list(group.values())
    for copy in every:
        copy.wait_send()


def per_device(*args):
    latents, step_noise, base_qkv, down_qkv, up_qkv, base_out, down_out, up_out, modulation, step = (
        args
    )
    n_fsdp, n_sp = lax.axis_size("fsdp"), lax.axis_size("sp")
    _, rows, d_model = latents.shape
    heads_here = base_qkv.shape[2] // HEAD_DIM
    tokens = rows * n_sp
    if n_sp != 2 or n_fsdp != 4 * PLANE or heads_here % PLANE or tokens % 16:
        return gather_weights(*args)
    n_z, n_head = n_fsdp // PLANE, heads_here // PLANE
    block = d_model // n_z
    half = block // 2
    w_rows = base_qkv.shape[1]
    width = 3 * HEAD_DIM
    cols = base_qkv.shape[2]
    f32, bf16 = jnp.float32, jnp.bfloat16
    if half % HEAD_DIM or w_rows % 32 or block != PLANE * w_rows or base_out.shape[1] != w_rows:
        return gather_weights(*args)
    padded = -(-rows // 16) * 16
    dma = pltpu.SemaphoreType.DMA
    vmem = pl.BlockSpec(memory_space=pltpu.VMEM)
    velocity, next_rows = pl.pallas_call(
        functools.partial(plane_kernel, n_z),
        out_shape=[jax.ShapeDtypeStruct((rows, d_model), bf16)] * 2,
        in_specs=[pl.BlockSpec(memory_space=pltpu.SMEM)] + [vmem] * 9,
        out_specs=[vmem] * 2,
        scratch_shapes=[
            pltpu.VMEM((2, rows, d_model), f32),
            pltpu.VMEM((tokens, d_model), bf16),
            pltpu.VMEM((2, n_z, PLANE, tokens, half), bf16),
            pltpu.VMEM((n_head, PLANE, w_rows, width), bf16),
            pltpu.VMEM((n_head, PLANE, w_rows, width), bf16),
            pltpu.VMEM((n_head, 3, PLANE * tokens, width), bf16),
            pltpu.VMEM((n_head, 3, PLANE * tokens, width), bf16),
            pltpu.VMEM((n_head, 2, PLANE * tokens, width), f32),
            pltpu.VMEM((n_head, PLANE, tokens, HEAD_DIM), bf16),
            pltpu.VMEM((n_z, tokens, cols), bf16),
            pltpu.VMEM((PLANE, w_rows, cols), bf16),
            pltpu.VMEM((2, n_z, rows, block), f32),
            pltpu.VMEM((n_z, rows, block), f32),
            pltpu.VMEM((n_z, padded, block), bf16),
            pltpu.VMEM((n_z, padded, block), bf16),
            dma((2,)),
            dma((2, n_z - 1)),
            dma((2, PLANE - 1)),
            dma((2, PLANE)),
            dma((2, n_head, PLANE - 1)),
            dma((2, n_head, 2)),
            dma((2, n_head)),
            dma((2, 3, 2)),
            dma((2, n_head, PLANE - 1)),
            dma((2, n_head, n_z - 1)),
            dma((2,)),
            dma((2, n_z - 1)),
        ],
        compiler_params=pltpu.CompilerParams(
            collective_id=0, has_side_effects=True, vmem_limit_bytes=48 * 1024 * 1024
        ),
        cost_estimate=pl.CostEstimate(
            flops=2 * n_fsdp * tokens * w_rows * 4 * cols,
            bytes_accessed=8 * w_rows * cols,
            transcendentals=0,
        ),
    )(
        step,
        latents[0],
        step_noise[0],
        base_qkv,
        down_qkv.swapaxes(1, 2),
        up_qkv,
        base_out.T,
        down_out.T,
        up_out,
        modulation.swapaxes(0, 1),
    )
    return (velocity[None], next_rows[None])


def gather_weights(
    latents,
    step_noise,
    base_qkv,
    down_qkv,
    up_query_key_value,
    base_out,
    down_out,
    up_out,
    modulation,
    timestep,
):
    step_index = timestep[0]
    mod_rows = lax.dynamic_index_in_dim(modulation, step_index, 0, keepdims=False)
    latent_f = latents[0].astype(jnp.float32)
    mean_square = jnp.mean(latent_f * latent_f, axis=-1, keepdims=True)
    normalized_rows = (
        latent_f * lax.rsqrt(mean_square + EPSILON) * (1.0 + mod_rows[1]) + mod_rows[0]
    ).astype(jnp.bfloat16)
    head_cols = base_qkv.shape[2]
    seq_len = normalized_rows.shape[0] * lax.axis_size("sp")
    every_token = lax.all_gather(normalized_rows, "sp", axis=0, tiled=True)
    lowrank = jnp.einsum(
        "prk,pkc->prc", down_qkv, up_query_key_value, preferred_element_type=jnp.float32
    )
    merged_qkv = (base_qkv.astype(jnp.float32) + lowrank).astype(jnp.bfloat16)
    projected = jnp.einsum(
        "lr,prc->plc",
        every_token,
        lax.all_gather(merged_qkv, "fsdp", axis=1, tiled=True),
        preferred_element_type=jnp.float32,
    ).astype(jnp.bfloat16)
    heads_here = head_cols // HEAD_DIM
    split_heads = projected.reshape(3, seq_len, heads_here, HEAD_DIM).transpose(2, 0, 1, 3)

    def one_head(triple):
        scores = jnp.dot(triple[0], triple[1].T, preferred_element_type=jnp.float32) * (
            1.0 / HEAD_DIM**0.5
        )
        attention_weights = jax.nn.softmax(scores, axis=-1).astype(jnp.bfloat16)
        return jnp.dot(attention_weights, triple[2], preferred_element_type=jnp.float32).astype(
            jnp.bfloat16
        )

    per_head = lax.map(one_head, split_heads)
    attention_result = per_head.transpose(1, 0, 2).reshape(seq_len, head_cols)
    merged_out = (
        base_out.astype(jnp.float32) + jnp.dot(down_out, up_out, preferred_element_type=jnp.float32)
    ).astype(jnp.bfloat16)
    full_out = lax.all_gather(merged_out, "fsdp", axis=1, tiled=True)
    block_out = lax.psum_scatter(
        jnp.dot(attention_result, full_out, preferred_element_type=jnp.float32).astype(
            jnp.bfloat16
        ),
        "sp",
        scatter_dimension=0,
        tiled=True,
    ).astype(jnp.float32)
    velocity = ((1.0 + mod_rows[2]) * block_out).astype(jnp.bfloat16)
    position = step_index.astype(jnp.float32)
    step_size = plan_sigma(position + 1.0) - plan_sigma(position)
    next_rows = (
        latent_f
        + step_size * velocity.astype(jnp.float32)
        + NOISE_LEVEL * jnp.sqrt(-step_size) * step_noise[0].astype(jnp.float32)
    )
    return (velocity[None], next_rows.astype(jnp.bfloat16)[None])


def solution(mesh):
    in_specs = (
        P("fsdp", "sp", None),
        P("fsdp", "sp", None),
        P(None, "fsdp", "sp"),
        P(None, "fsdp", None),
        P(None, None, "sp"),
        P("sp", "fsdp"),
        P("sp", None),
        P(None, "fsdp"),
        P(),
        P("fsdp"),
    )
    out_specs = (P("fsdp", "sp", None), P("fsdp", "sp", None))
    return jax.shard_map(
        per_device, mesh=mesh, in_specs=in_specs, out_specs=out_specs, check_vma=False
    )
```

```python
import functools

import jax
import jax.numpy as jnp
from jax import lax
from jax.experimental import pallas as pl
from jax.experimental.pallas import tpu as pltpu
from jax.sharding import PartitionSpec as P

HEAD_DIM = 128
NSTEP = 16


EPSILON = 1e-06
SHIFT_FACTOR = 5.0
NOISE_LEVEL = 0.7


def plan_sigma(position):
    ramp = 1.0 - position / NSTEP
    return SHIFT_FACTOR * ramp / (1.0 + (SHIFT_FACTOR - 1.0) * ramp)


PLANE = 4
MESH = pl.DeviceIdType.MESH


def plane_kernel(
    n_z,
    step_ref,
    latents_hbm,
    noise_hbm,
    base_qkv_hbm,
    down_qkv_hbm,
    up_qkv_hbm,
    base_out_hbm,
    down_out_hbm,
    up_out_hbm,
    mod_hbm,
    velocity_ref,
    next_ref,
    latents_ref,
    noise_ref,
    base_qkv_ref,
    down_qkv_ref,
    up_qkv_ref,
    base_out_ref,
    down_out_ref,
    up_out_ref,
    mod_ref,
    in_sem,
    latf,
    normed,
    acts,
    w_send,
    w_recv,
    part_send,
    part_recv,
    part_own,
    att_send,
    att_all,
    wo_all,
    out_half,
    out_sib,
    vel_send,
    vel_recv,
    lat_sem,
    x1_sem,
    x3_sem,
    xs_sem,
    w_sem,
    pair_sem,
    far_sem,
    wo_sem,
    at_sem,
    ag_sem,
    os_sem,
    v_sem,
):
    loads = {}
    for k, (source, target) in enumerate(
        (
            (latents_hbm, latents_ref),
            (base_qkv_hbm, base_qkv_ref),
            (down_qkv_hbm, down_qkv_ref),
            (up_qkv_hbm, up_qkv_ref),
            (mod_hbm, mod_ref),
            (base_out_hbm, base_out_ref),
            (down_out_hbm, down_out_ref),
            (up_out_hbm, up_out_ref),
            (noise_hbm, noise_ref),
        )
    ):
        loads[k] = pltpu.make_async_copy(source, target, in_sem.at[k])
        loads[k].start()
    f, c = lax.axis_index("fsdp"), lax.axis_index("sp")
    z, j = f // PLANE, f % PLANE
    rows, d_model = latents_ref.shape
    tokens = 2 * rows
    n_head = w_send.shape[0]
    block = d_model // n_z
    half = block // 2
    w_rows = base_qkv_ref.shape[1]
    x_at, y_at = j % 2, j // 2
    z_lo, z_hi = z % 2, z // 2
    x_near, y_near = 2 * y_at + 1 - x_at, 2 * (1 - y_at) + x_at
    width = 3 * HEAD_DIM
    f32, bf16 = jnp.float32, jnp.bfloat16

    def in_plane(d):
        return (z * PLANE + (j + d) % PLANE, c)

    def in_column(d):
        return (((z + d) % n_z) * PLANE + j, c)

    sibling = (f, 1 - c)
    x_device, y_device = (z * PLANE + x_near, c), (z * PLANE + y_near, c)
    z_pair = ((2 * z_hi + 1 - z_lo) * PLANE + j, c)
    z_far = ((2 * (1 - z_hi) + z_lo) * PLANE + j, c)

    def send(src, dst, sems, where, device):
        copy = pltpu.make_async_remote_copy(
            src_ref=src,
            dst_ref=dst,
            send_sem=sems.at[(0, *where)],
            recv_sem=sems.at[(1, *where)],
            device_id=device,
            device_id_type=MESH,
        )
        copy.start()
        return copy

    barrier = pltpu.get_barrier_semaphore()
    partners = [sibling]
    partners += [in_plane(d) for d in range(1, PLANE)]
    partners += [in_column(d) for d in range(1, n_z)]
    for partner in partners:
        pl.semaphore_signal(barrier, inc=1, device_id=partner, device_id_type=MESH)

    loads[0].wait()
    latf[c] = latents_ref[...].astype(f32)

    def merge(h):
        for g in range(PLANE):
            at = (g * n_head + h) * HEAD_DIM
            for p in range(3):
                lowrank = lax.dot_general(
                    down_qkv_ref[p],
                    up_qkv_ref[p, :, at : at + HEAD_DIM],
                    (((0,), (0,)), ((), ())),
                    preferred_element_type=f32,
                )
                w_send[h, g, :, p * HEAD_DIM : (p + 1) * HEAD_DIM] = (
                    base_qkv_ref[p, :, at : at + HEAD_DIM].astype(f32) + lowrank
                ).astype(bf16)
        w_recv[h, j] = w_send[h, j]

    pl.semaphore_wait(barrier, len(partners))
    lat_copy = send(latf.at[c], latf.at[c], lat_sem, (), sibling)
    w_copies = {}

    def send_weights(h):
        for d in range(1, PLANE):
            w_copies[h, d] = send(
                w_send.at[h, (j + d) % PLANE], w_recv.at[h, j], w_sem, (h, d - 1), in_plane(d)
            )

    for k in (1, 2, 3):
        loads[k].wait()
    merge(0)
    send_weights(0)

    step_index = step_ref[0]
    loads[4].wait()

    def mod_row(k):
        return mod_ref[k, pl.ds(step_index, 1), :]

    lat_copy.wait_recv()
    lat_rows = latf[...].reshape(tokens, d_model)
    mean_square = jnp.mean(lat_rows * lat_rows, axis=-1, keepdims=True)
    normed[...] = (
        lat_rows * lax.rsqrt(mean_square + EPSILON) * (1.0 + mod_row(1)) + mod_row(0)
    ).astype(bf16)

    def features(z_at):
        return pl.ds(pl.multiple_of(z_at * block + c * half, half), half)

    x1 = [
        send(
            normed.at[:, features((z + d) % n_z)],
            acts.at[c, z, j],
            x1_sem,
            (d - 1,),
            in_column(d),
        )
        for d in range(1, n_z)
    ]
    acts[c, z, j] = normed[:, features(z)]
    if n_head > 1:
        merge(1)
    for copy in x1:
        copy.wait_recv()
    x3 = [
        send(acts.at[c, :, j], acts.at[c, :, j], x3_sem, (d - 1,), in_plane(d))
        for d in range(1, PLANE)
    ]
    xs = [send(acts.at[c, :, j], acts.at[c, :, j], xs_sem, (0,), sibling)]
    for h in range(2, n_head):
        merge(h)
    for k in (5, 6, 7):
        loads[k].wait()
    merged_out = (
        base_out_ref[...].astype(f32)
        + lax.dot_general(
            up_out_ref[...],
            down_out_ref[...],
            (((0,), (0,)), ((), ())),
            preferred_element_type=f32,
        )
    ).astype(bf16)
    for g in range(PLANE):
        for h in range(n_head):
            at, to = (g * n_head + h) * HEAD_DIM, (h * PLANE + g) * HEAD_DIM
            wo_all[j, :, to : to + HEAD_DIM] = merged_out[:, at : at + HEAD_DIM]
    for d in range(1, PLANE):
        x3[d - 1].wait_recv()
        came = (j + PLANE - d) % PLANE
        xs.append(send(acts.at[c, :, came], acts.at[c, :, came], xs_sem, (d,), sibling))
    if n_head > 1:
        send_weights(1)
    for copy in xs:
        copy.wait_recv()

    wo_x, wo_y, wo_far = [], [], []
    wo_half = w_rows // 2

    def send_out_rows(owner, k, where, device):
        view = wo_all.at[owner, pl.ds(k * wo_half, wo_half)]
        return send(view, view, wo_sem, where, device)

    pair_copies, far_copies = {}, {}
    def partial_sums(h):
        for d in range(1, PLANE):
            w_copies[h, d].wait_recv()
        if h == n_head - 1:
            for k in range(2):
                wo_x.append(send_out_rows(j, k, (0, k), x_device))
                wo_y.append(send_out_rows(j, 1 - k, (1, 1 - k), y_device))
        weights = w_recv[h].reshape(PLANE * w_rows, width)
        for parity, hi in ((1, 1), (1, 0), (0, 1), (0, 0)):
            z_at = 2 * ((z_hi + hi) % 2) + (z_lo + parity) % 2
            part = jnp.dot(
                acts[0, z_at].reshape(PLANE * tokens, half),
                weights[:half],
                preferred_element_type=f32,
            ) + jnp.dot(
                acts[1, z_at].reshape(PLANE * tokens, half),
                weights[half:],
                preferred_element_type=f32,
            )
            if parity:
                part_send[h, hi] = part.astype(bf16)
                pair_copies[h, hi] = send(
                    part_send.at[h, hi], part_recv.at[h, hi], pair_sem, (h, hi), z_pair
                )
            else:
                part_own[h, hi] = part

    def send_far(h):
        pair_copies[h, 1].wait_recv()
        part_send[h, 2] = (part_own[h, 1] + part_recv[h, 1].astype(f32)).astype(bf16)
        far_copies[h] = send(part_send.at[h, 2], part_recv.at[h, 2], far_sem, (h,), z_far)

    at_copies, ag_copies = {}, {}

    def lanes(h, g):
        return pl.ds(pl.multiple_of((h * PLANE + g) * HEAD_DIM, HEAD_DIM), HEAD_DIM)

    def spread(h):
        for d in range(1, PLANE):
            at_copies[h, d].wait_recv()
        chunk = pl.ds(h * PLANE * HEAD_DIM, PLANE * HEAD_DIM)
        for d in range(1, n_z):
            ag_copies[h, d] = send(
                att_all.at[z, :, chunk],
                att_all.at[z, :, chunk],
                ag_sem,
                (h, d - 1),
                in_column(d),
            )

    def attend(h):
        pair_copies[h, 0].wait_recv()
        far_copies[h].wait_recv()
        projected = (
            part_own[h, 0] + part_recv[h, 0].astype(f32) + part_recv[h, 2].astype(f32)
        ).astype(bf16)
        for s in range(PLANE):
            rows_s = projected[s * tokens : (s + 1) * tokens]
            query = rows_s[:, :HEAD_DIM]
            key = rows_s[:, HEAD_DIM : 2 * HEAD_DIM]
            value = rows_s[:, 2 * HEAD_DIM :]
            scores = lax.dot_general(
                query, key, (((1,), (1,)), ((), ())), preferred_element_type=f32
            ) * (1.0 / HEAD_DIM**0.5)
            weights = jnp.exp(scores - jnp.max(scores, axis=-1, keepdims=True))
            weights = weights / jnp.sum(weights, axis=-1, keepdims=True)
            att_send[h, s] = jnp.dot(
                weights.astype(bf16), value, preferred_element_type=f32
            ).astype(bf16)
        for d in range(1, PLANE):
            at_copies[h, d] = send(
                att_send.at[h, (j + d) % PLANE],
                att_all.at[z, :, lanes(h, j)],
                at_sem,
                (h, d - 1),
                in_plane(d),
            )
        att_all[z, :, lanes(h, j)] = att_send[h, j]

    for h in range(n_head):
        partial_sums(h)
        if h + 2 < n_head:
            send_weights(h + 2)
        if h:
            send_far(h - 1)
        if h > 1:
            attend(h - 2)
    send_far(n_head - 1)
    for h in range(max(n_head - 2, 0), n_head):
        if h:
            spread(h - 1)
        attend(h)
    wo_x[0].wait_recv()
    wo_far.append(send_out_rows(x_near, 0, (2, 0), y_device))
    wo_y[0].wait_recv()
    wo_far.append(send_out_rows(y_near, 1, (2, 1), x_device))
    spread(n_head - 1)

    for copy in (wo_x[1], wo_y[1], *wo_far):
        copy.wait_recv()
    out = None
    for h in range(n_head):
        for d in range(1, n_z):
            ag_copies[h, d].wait_recv()
        chunk = slice(h * PLANE * HEAD_DIM, (h + 1) * PLANE * HEAD_DIM)
        term = lax.dot_general(
            att_all[:, :, chunk].reshape(n_z * tokens, PLANE * HEAD_DIM),
            wo_all[:, :, chunk].reshape(block, PLANE * HEAD_DIM),
            (((1,), (1,)), ((), ())),
            preferred_element_type=f32,
        )
        out = term if out is None else out + term
    for s in range(n_z):
        for k in range(2):
            at = s * tokens + k * rows
            out_half[k, s] = out[at : at + rows]
    os_copy = send(out_half.at[1 - c], out_sib, os_sem, (), sibling)
    os_copy.wait_recv()
    pad = jnp.zeros((vel_send.shape[1] - rows, block), f32)
    v_copies = []
    for d in list(range(1, n_z)) + [0]:
        z_at = (z + d) % n_z
        block_sum = out_half[c, z_at] + out_sib[z_at]
        block_sum = jnp.concatenate([block_sum, pad], axis=0).astype(bf16)
        if d:
            vel_send[z_at] = block_sum
            v_copies.append(
                send(vel_send.at[z_at], vel_recv.at[z], v_sem, (d - 1,), in_column(d))
            )
        else:
            vel_recv[z] = block_sum

    gate = mod_row(2)
    loads[8].wait()
    position = jnp.full((1, block), step_index.astype(f32), f32)
    step_size = plan_sigma(position + 1.0) - plan_sigma(position)
    noise_size = NOISE_LEVEL * jnp.sqrt(-step_size)
    for copy in v_copies:
        copy.wait_recv()
    for s in range(n_z):
        cols = slice(s * block, (s + 1) * block)
        block_out = vel_recv[s].astype(f32)[:rows]
        velocity = ((1.0 + gate[:, cols]) * block_out).astype(bf16)
        velocity_ref[:, cols] = velocity
        next_ref[:, cols] = (
            latf[c, :, cols]
            + step_size * velocity.astype(f32)
            + noise_size * noise_ref[:, cols].astype(f32)
        ).astype(bf16)

    every = [lat_copy, os_copy, *x1, *x3, *xs, *wo_x, *wo_y, *wo_far, *v_copies]
    for group in (w_copies, pair_copies, far_copies, at_copies, ag_copies):
        every += list(group.values())
    for copy in every:
        copy.wait_send()


def per_device(*args):
    latents, step_noise, base_qkv, down_qkv, up_qkv, base_out, down_out, up_out, modulation, step = (
        args
    )
    n_fsdp, n_sp = lax.axis_size("fsdp"), lax.axis_size("sp")
    _, rows, d_model = latents.shape
    heads_here = base_qkv.shape[2] // HEAD_DIM
    tokens = rows * n_sp
    if n_sp != 2 or n_fsdp != 4 * PLANE or heads_here % PLANE or tokens % 16:
        return gather_weights(*args)
    n_z, n_head = n_fsdp // PLANE, heads_here // PLANE
    block = d_model // n_z
    half = block // 2
    w_rows = base_qkv.shape[1]
    width = 3 * HEAD_DIM
    cols = base_qkv.shape[2]
    f32, bf16 = jnp.float32, jnp.bfloat16
    if half % HEAD_DIM or w_rows % 32 or block != PLANE * w_rows or base_out.shape[1] != w_rows:
        return gather_weights(*args)
    operands = (
        base_qkv,
        down_qkv.swapaxes(1, 2),
        up_qkv,
        base_out.T,
        down_out.T,
        up_out,
        modulation.swapaxes(0, 1),
    )
    padded = -(-rows // 16) * 16
    dma = pltpu.SemaphoreType.DMA
    vmem = pl.BlockSpec(memory_space=pltpu.VMEM)
    velocity, next_rows = pl.pallas_call(
        functools.partial(plane_kernel, n_z),
        out_shape=[jax.ShapeDtypeStruct((rows, d_model), bf16)] * 2,
        in_specs=[pl.BlockSpec(memory_space=pltpu.SMEM)] + [pl.BlockSpec(memory_space=pl.ANY)] * 9,
        out_specs=[vmem] * 2,
        scratch_shapes=[
            pltpu.VMEM(latents.shape[1:], bf16),
            pltpu.VMEM(step_noise.shape[1:], bf16),
            *[pltpu.VMEM(array.shape, array.dtype) for array in operands],
            dma((9,)),
            pltpu.VMEM((2, rows, d_model), f32),
            pltpu.VMEM((tokens, d_model), bf16),
            pltpu.VMEM((2, n_z, PLANE, tokens, half), bf16),
            pltpu.VMEM((n_head, PLANE, w_rows, width), bf16),
            pltpu.VMEM((n_head, PLANE, w_rows, width), bf16),
            pltpu.VMEM((n_head, 3, PLANE * tokens, width), bf16),
            pltpu.VMEM((n_head, 3, PLANE * tokens, width), bf16),
            pltpu.VMEM((n_head, 2, PLANE * tokens, width), f32),
            pltpu.VMEM((n_head, PLANE, tokens, HEAD_DIM), bf16),
            pltpu.VMEM((n_z, tokens, cols), bf16),
            pltpu.VMEM((PLANE, w_rows, cols), bf16),
            pltpu.VMEM((2, n_z, rows, block), f32),
            pltpu.VMEM((n_z, rows, block), f32),
            pltpu.VMEM((n_z, padded, block), bf16),
            pltpu.VMEM((n_z, padded, block), bf16),
            dma((2,)),
            dma((2, n_z - 1)),
            dma((2, PLANE - 1)),
            dma((2, PLANE)),
            dma((2, n_head, PLANE - 1)),
            dma((2, n_head, 2)),
            dma((2, n_head)),
            dma((2, 3, 2)),
            dma((2, n_head, PLANE - 1)),
            dma((2, n_head, n_z - 1)),
            dma((2,)),
            dma((2, n_z - 1)),
        ],
        compiler_params=pltpu.CompilerParams(
            collective_id=0, has_side_effects=True, vmem_limit_bytes=56 * 1024 * 1024
        ),
        cost_estimate=pl.CostEstimate(
            flops=2 * n_fsdp * tokens * w_rows * 4 * cols,
            bytes_accessed=8 * w_rows * cols,
            transcendentals=0,
        ),
    )(
        step,
        latents[0],
        step_noise[0],
        *operands,
    )
    return (velocity[None], next_rows[None])


def gather_weights(
    latents,
    step_noise,
    base_qkv,
    down_qkv,
    up_query_key_value,
    base_out,
    down_out,
    up_out,
    modulation,
    timestep,
):
    step_index = timestep[0]
    mod_rows = lax.dynamic_index_in_dim(modulation, step_index, 0, keepdims=False)
    latent_f = latents[0].astype(jnp.float32)
    mean_square = jnp.mean(latent_f * latent_f, axis=-1, keepdims=True)
    normalized_rows = (
        latent_f * lax.rsqrt(mean_square + EPSILON) * (1.0 + mod_rows[1]) + mod_rows[0]
    ).astype(jnp.bfloat16)
    head_cols = base_qkv.shape[2]
    seq_len = normalized_rows.shape[0] * lax.axis_size("sp")
    every_token = lax.all_gather(normalized_rows, "sp", axis=0, tiled=True)
    lowrank = jnp.einsum(
        "prk,pkc->prc", down_qkv, up_query_key_value, preferred_element_type=jnp.float32
    )
    merged_qkv = (base_qkv.astype(jnp.float32) + lowrank).astype(jnp.bfloat16)
    projected = jnp.einsum(
        "lr,prc->plc",
        every_token,
        lax.all_gather(merged_qkv, "fsdp", axis=1, tiled=True),
        preferred_element_type=jnp.float32,
    ).astype(jnp.bfloat16)
    heads_here = head_cols // HEAD_DIM
    split_heads = projected.reshape(3, seq_len, heads_here, HEAD_DIM).transpose(2, 0, 1, 3)

    def one_head(triple):
        scores = jnp.dot(triple[0], triple[1].T, preferred_element_type=jnp.float32) * (
            1.0 / HEAD_DIM**0.5
        )
        attention_weights = jax.nn.softmax(scores, axis=-1).astype(jnp.bfloat16)
        return jnp.dot(attention_weights, triple[2], preferred_element_type=jnp.float32).astype(
            jnp.bfloat16
        )

    per_head = lax.map(one_head, split_heads)
    attention_result = per_head.transpose(1, 0, 2).reshape(seq_len, head_cols)
    merged_out = (
        base_out.astype(jnp.float32) + jnp.dot(down_out, up_out, preferred_element_type=jnp.float32)
    ).astype(jnp.bfloat16)
    full_out = lax.all_gather(merged_out, "fsdp", axis=1, tiled=True)
    block_out = lax.psum_scatter(
        jnp.dot(attention_result, full_out, preferred_element_type=jnp.float32).astype(
            jnp.bfloat16
        ),
        "sp",
        scatter_dimension=0,
        tiled=True,
    ).astype(jnp.float32)
    velocity = ((1.0 + mod_rows[2]) * block_out).astype(jnp.bfloat16)
    position = step_index.astype(jnp.float32)
    step_size = plan_sigma(position + 1.0) - plan_sigma(position)
    next_rows = (
        latent_f
        + step_size * velocity.astype(jnp.float32)
        + NOISE_LEVEL * jnp.sqrt(-step_size) * step_noise[0].astype(jnp.float32)
    )
    return (velocity[None], next_rows.astype(jnp.bfloat16)[None])


def solution(mesh):
    in_specs = (
        P("fsdp", "sp", None),
        P("fsdp", "sp", None),
        P(None, "fsdp", "sp"),
        P(None, "fsdp", None),
        P(None, None, "sp"),
        P("sp", "fsdp"),
        P("sp", None),
        P(None, "fsdp"),
        P(),
        P("fsdp"),
    )
    out_specs = (P("fsdp", "sp", None), P("fsdp", "sp", None))
    return jax.shard_map(
        per_device, mesh=mesh, in_specs=in_specs, out_specs=out_specs, check_vma=False
    )
```

```python
import functools

import jax
import jax.numpy as jnp
from jax import lax
from jax.experimental import pallas as pl
from jax.experimental.pallas import tpu as pltpu
from jax.sharding import PartitionSpec as P

HEAD_DIM = 128
NSTEP = 16


EPSILON = 1e-06
SHIFT_FACTOR = 5.0
NOISE_LEVEL = 0.7


def plan_sigma(position):
    ramp = 1.0 - position / NSTEP
    return SHIFT_FACTOR * ramp / (1.0 + (SHIFT_FACTOR - 1.0) * ramp)


PLANE = 4
MESH = pl.DeviceIdType.MESH


def plane_kernel(
    n_z,
    step_ref,
    latents_hbm,
    base_qkv_hbm,
    down_qkv_hbm,
    up_qkv_hbm,
    base_out_hbm,
    down_out_hbm,
    up_out_hbm,
    mod_hbm,
    result_ref,
    factors_ref,
    latents_ref,
    up_qkv_ref,
    base_out_ref,
    down_out_ref,
    up_out_ref,
    mod_ref,
    in_sem,
    latf,
    normed,
    acts,
    base_all,
    down_all,
    lowrank,
    w_all,
    part_send,
    part_recv,
    part_own,
    att_send,
    att_all,
    wo_all,
    out_half,
    out_sib,
    vel_send,
    vel_recv,
    lat_sem,
    x1_sem,
    x3_sem,
    xs_sem,
    w_sem,
    down_sem,
    pair_sem,
    far_sem,
    wo_sem,
    at_sem,
    ag_sem,
    os_sem,
    v_sem,
):
    f, c = lax.axis_index("fsdp"), lax.axis_index("sp")
    z, j = f // PLANE, f % PLANE
    rows, d_model = latents_ref.shape
    tokens = 2 * rows
    n_head = w_all.shape[0]
    own = n_head * HEAD_DIM
    own_cols = pl.ds(pl.multiple_of(j * own, HEAD_DIM), own)
    block = d_model // n_z
    half = block // 2
    w_rows = base_qkv_hbm.shape[1]
    x_at, y_at = j % 2, j // 2
    z_lo, z_hi = z % 2, z // 2
    x_near, y_near = 2 * y_at + 1 - x_at, 2 * (1 - y_at) + x_at
    width = 3 * HEAD_DIM
    f32, bf16 = jnp.float32, jnp.bfloat16

    def in_plane(d):
        return (z * PLANE + (j + d) % PLANE, c)

    def in_column(d):
        return (((z + d) % n_z) * PLANE + j, c)

    sibling = (f, 1 - c)
    x_device, y_device = (z * PLANE + x_near, c), (z * PLANE + y_near, c)
    z_pair = ((2 * z_hi + 1 - z_lo) * PLANE + j, c)
    z_far = ((2 * (1 - z_hi) + z_lo) * PLANE + j, c)

    def send(src, dst, sems, where, device):
        copy = pltpu.make_async_remote_copy(
            src_ref=src,
            dst_ref=dst,
            send_sem=sems.at[(0, *where)],
            recv_sem=sems.at[(1, *where)],
            device_id=device,
            device_id_type=MESH,
        )
        copy.start()
        return copy

    loads = {}
    for k, (source, target) in enumerate(
        (
            (latents_hbm, latents_ref),
            (base_qkv_hbm.at[:, :, own_cols], base_all.at[:, j]),
            (down_qkv_hbm, down_all.at[j]),
            (up_qkv_hbm.at[:, :, own_cols], up_qkv_ref),
            (mod_hbm, mod_ref),
            (base_out_hbm, base_out_ref),
            (down_out_hbm, down_out_ref),
            (up_out_hbm, up_out_ref),
        )
    ):
        loads[k] = pltpu.make_async_copy(source, target, in_sem.at[k])
        loads[k].start()
    barrier = pltpu.get_barrier_semaphore()
    partners = [sibling]
    partners += [in_plane(d) for d in range(1, PLANE)]
    partners += [in_column(d) for d in range(1, n_z)]
    for partner in partners:
        pl.semaphore_signal(barrier, inc=1, device_id=partner, device_id_type=MESH)

    loads[0].wait()
    latf[c] = latents_ref[...].astype(f32)

    pl.semaphore_wait(barrier, len(partners))
    lat_copy = send(latf.at[c], latf.at[c], lat_sem, (), sibling)
    w_copies = {}

    def send_weights(h):
        lanes_h = slice(h * HEAD_DIM, (h + 1) * HEAD_DIM)
        for d in range(1, PLANE):
            at = ((j + d) % PLANE) * own + h * HEAD_DIM
            cols = pl.ds(pl.multiple_of(at, HEAD_DIM), HEAD_DIM)
            for p in range(3):
                w_copies[h, d, p] = send(
                    base_qkv_hbm.at[p, :, cols],
                    base_all.at[p, j, :, lanes_h],
                    w_sem,
                    (h, d - 1, p),
                    in_plane(d),
                )

    send_weights(0)
    loads[2].wait()
    down_copies = [
        send(down_all.at[j], down_all.at[j], down_sem, (d - 1,), in_plane(d))
        for d in range(1, PLANE)
    ]

    step_index = step_ref[0]
    loads[4].wait()

    def mod_row(k):
        return mod_ref[k, pl.ds(step_index, 1), :]

    lat_copy.wait_recv()
    lat_rows = latf[...].reshape(tokens, d_model)
    mean_square = jnp.mean(lat_rows * lat_rows, axis=-1, keepdims=True)
    normed[...] = (
        lat_rows * lax.rsqrt(mean_square + EPSILON) * (1.0 + mod_row(1)) + mod_row(0)
    ).astype(bf16)

    def features(z_at):
        return pl.ds(pl.multiple_of(z_at * block + c * half, half), half)

    x1 = [
        send(
            normed.at[:, features((z + d) % n_z)],
            acts.at[c, z, j],
            x1_sem,
            (d - 1,),
            in_column(d),
        )
        for d in range(1, n_z)
    ]
    acts[c, z, j] = normed[:, features(z)]
    for copy in x1:
        copy.wait_recv()
    x3 = [
        send(acts.at[c, :, j], acts.at[c, :, j], x3_sem, (d - 1,), in_plane(d))
        for d in range(1, PLANE)
    ]
    xs = [send(acts.at[c, :, j], acts.at[c, :, j], xs_sem, (0,), sibling)]
    for copy in down_copies:
        copy.wait_recv()
    for k in (1, 3):
        loads[k].wait()
    for p in range(3):
        for g in range(PLANE):
            lowrank[p, g] = lax.dot_general(
                down_all[g, p],
                up_qkv_ref[p],
                (((0,), (0,)), ((), ())),
                preferred_element_type=f32,
            )
    position = jnp.full((1, d_model), step_index.astype(f32), f32)
    step_size = plan_sigma(position + 1.0) - plan_sigma(position)
    factors_ref[...] = jnp.concatenate(
        [
            1.0 + mod_row(2),
            step_size,
            NOISE_LEVEL * jnp.sqrt(-step_size),
            jnp.zeros((factors_ref.shape[0] - 3, d_model), f32),
        ],
        axis=0,
    )
    for k in (5, 6, 7):
        loads[k].wait()
    merged_out = (
        base_out_ref[...].astype(f32)
        + lax.dot_general(
            up_out_ref[...],
            down_out_ref[...],
            (((0,), (0,)), ((), ())),
            preferred_element_type=f32,
        )
    ).astype(bf16)
    for g in range(PLANE):
        for h in range(n_head):
            at, to = (g * n_head + h) * HEAD_DIM, (h * PLANE + g) * HEAD_DIM
            wo_all[j, :, to : to + HEAD_DIM] = merged_out[:, at : at + HEAD_DIM]
    for d in range(1, PLANE):
        x3[d - 1].wait_recv()
        came = (j + PLANE - d) % PLANE
        xs.append(send(acts.at[c, :, came], acts.at[c, :, came], xs_sem, (d,), sibling))
    if n_head > 1:
        send_weights(1)
    for copy in xs:
        copy.wait_recv()

    wo_x, wo_y, wo_far = [], [], []
    wo_half = w_rows // 2

    def send_out_rows(owner, k, where, device):
        view = wo_all.at[owner, pl.ds(k * wo_half, wo_half)]
        return send(view, view, wo_sem, where, device)

    pair_copies, far_copies = {}, {}
    def partial_sums(h):
        for d in range(1, PLANE):
            for p in range(3):
                w_copies[h, d, p].wait_recv()
        if h == n_head - 1:
            for k in range(2):
                wo_x.append(send_out_rows(j, k, (0, k), x_device))
                wo_y.append(send_out_rows(j, 1 - k, (1, 1 - k), y_device))
        lanes_h = slice(h * HEAD_DIM, (h + 1) * HEAD_DIM)
        for p in range(3):
            merged = (base_all[p, :, :, lanes_h].astype(f32) + lowrank[p, :, :, lanes_h]).astype(bf16)
            w_all[h, :, p * HEAD_DIM : (p + 1) * HEAD_DIM] = merged.reshape(
                PLANE * w_rows, HEAD_DIM
            )
        weights = w_all[h]
        for parity, hi in ((1, 1), (1, 0), (0, 1), (0, 0)):
            z_at = 2 * ((z_hi + hi) % 2) + (z_lo + parity) % 2
            part = jnp.dot(
                acts[0, z_at].reshape(PLANE * tokens, half),
                weights[:half],
                preferred_element_type=f32,
            ) + jnp.dot(
                acts[1, z_at].reshape(PLANE * tokens, half),
                weights[half:],
                preferred_element_type=f32,
            )
            if parity:
                part_send[h, hi] = part.astype(bf16)
                pair_copies[h, hi] = send(
                    part_send.at[h, hi], part_recv.at[h, hi], pair_sem, (h, hi), z_pair
                )
            else:
                part_own[h, hi] = part

    def send_far(h):
        pair_copies[h, 1].wait_recv()
        part_send[h, 2] = (part_own[h, 1] + part_recv[h, 1].astype(f32)).astype(bf16)
        far_copies[h] = send(part_send.at[h, 2], part_recv.at[h, 2], far_sem, (h,), z_far)

    at_copies, ag_copies = {}, {}

    def lanes(h, g):
        return pl.ds(pl.multiple_of((h * PLANE + g) * HEAD_DIM, HEAD_DIM), HEAD_DIM)

    def spread(h):
        for d in range(1, PLANE):
            at_copies[h, d].wait_recv()
        chunk = pl.ds(h * PLANE * HEAD_DIM, PLANE * HEAD_DIM)
        for d in range(1, n_z):
            ag_copies[h, d] = send(
                att_all.at[z, :, chunk],
                att_all.at[z, :, chunk],
                ag_sem,
                (h, d - 1),
                in_column(d),
            )

    def attend(h):
        pair_copies[h, 0].wait_recv()
        far_copies[h].wait_recv()
        projected = (
            part_own[h, 0] + part_recv[h, 0].astype(f32) + part_recv[h, 2].astype(f32)
        ).astype(bf16)
        for s in range(PLANE):
            rows_s = projected[s * tokens : (s + 1) * tokens]
            query = rows_s[:, :HEAD_DIM]
            key = rows_s[:, HEAD_DIM : 2 * HEAD_DIM]
            value = rows_s[:, 2 * HEAD_DIM :]
            scores = lax.dot_general(
                query, key, (((1,), (1,)), ((), ())), preferred_element_type=f32
            ) * (1.0 / HEAD_DIM**0.5)
            weights = jnp.exp(scores - jnp.max(scores, axis=-1, keepdims=True))
            weights = weights / jnp.sum(weights, axis=-1, keepdims=True)
            att_send[h, s] = jnp.dot(
                weights.astype(bf16), value, preferred_element_type=f32
            ).astype(bf16)
        for d in range(1, PLANE):
            at_copies[h, d] = send(
                att_send.at[h, (j + d) % PLANE],
                att_all.at[z, :, lanes(h, j)],
                at_sem,
                (h, d - 1),
                in_plane(d),
            )
        att_all[z, :, lanes(h, j)] = att_send[h, j]

    for h in range(n_head):
        partial_sums(h)
        if h + 2 < n_head:
            send_weights(h + 2)
        if h:
            send_far(h - 1)
        if h > 1:
            attend(h - 2)
    send_far(n_head - 1)
    for h in range(max(n_head - 2, 0), n_head):
        if h:
            spread(h - 1)
        attend(h)
    wo_x[0].wait_recv()
    wo_far.append(send_out_rows(x_near, 0, (2, 0), y_device))
    wo_y[0].wait_recv()
    wo_far.append(send_out_rows(y_near, 1, (2, 1), x_device))
    spread(n_head - 1)

    for copy in (wo_x[1], wo_y[1], *wo_far):
        copy.wait_recv()
    out = None
    for h in range(n_head):
        for d in range(1, n_z):
            ag_copies[h, d].wait_recv()
        chunk = slice(h * PLANE * HEAD_DIM, (h + 1) * PLANE * HEAD_DIM)
        term = lax.dot_general(
            att_all[:, :, chunk].reshape(n_z * tokens, PLANE * HEAD_DIM),
            wo_all[:, :, chunk].reshape(block, PLANE * HEAD_DIM),
            (((1,), (1,)), ((), ())),
            preferred_element_type=f32,
        )
        out = term if out is None else out + term
    for s in range(n_z):
        for k in range(2):
            at = s * tokens + k * rows
            out_half[k, s] = out[at : at + rows]
    os_copy = send(out_half.at[1 - c], out_sib, os_sem, (), sibling)
    os_copy.wait_recv()
    pad = jnp.zeros((vel_send.shape[1] - rows, block), f32)
    v_copies = []
    for d in list(range(1, n_z)) + [0]:
        z_at = (z + d) % n_z
        block_sum = out_half[c, z_at] + out_sib[z_at]
        block_sum = jnp.concatenate([block_sum, pad], axis=0).astype(bf16)
        if d:
            vel_send[z_at] = block_sum
            v_copies.append(
                send(vel_send.at[z_at], vel_recv.at[z], v_sem, (d - 1,), in_column(d))
            )
        else:
            vel_recv[z] = block_sum

    for copy in v_copies:
        copy.wait_recv()
    for s in range(n_z):
        result_ref[:, s * block : (s + 1) * block] = vel_recv[s, :rows]

    every = [lat_copy, os_copy, *x1, *x3, *xs, *wo_x, *wo_y, *wo_far, *v_copies, *down_copies]
    for group in (w_copies, pair_copies, far_copies, at_copies, ag_copies):
        every += list(group.values())
    for copy in every:
        copy.wait_send()


def per_device(*args):
    latents, step_noise, base_qkv, down_qkv, up_qkv, base_out, down_out, up_out, modulation, step = (
        args
    )
    n_fsdp, n_sp = lax.axis_size("fsdp"), lax.axis_size("sp")
    _, rows, d_model = latents.shape
    heads_here = base_qkv.shape[2] // HEAD_DIM
    tokens = rows * n_sp
    if n_sp != 2 or n_fsdp != 4 * PLANE or heads_here % PLANE or tokens % 16:
        return gather_weights(*args)
    n_z, n_head = n_fsdp // PLANE, heads_here // PLANE
    block = d_model // n_z
    half = block // 2
    w_rows = base_qkv.shape[1]
    width = 3 * HEAD_DIM
    cols = base_qkv.shape[2]
    f32, bf16 = jnp.float32, jnp.bfloat16
    if half % HEAD_DIM or w_rows % 32 or block != PLANE * w_rows or base_out.shape[1] != w_rows:
        return gather_weights(*args)
    operands = (
        base_qkv,
        down_qkv.swapaxes(1, 2),
        up_qkv,
        base_out.T,
        down_out.T,
        up_out,
        modulation.swapaxes(0, 1),
    )
    padded = -(-rows // 16) * 16
    dma = pltpu.SemaphoreType.DMA
    vmem = pl.BlockSpec(memory_space=pltpu.VMEM)
    block_out, factors = pl.pallas_call(
        functools.partial(plane_kernel, n_z),
        out_shape=[
            jax.ShapeDtypeStruct((rows, d_model), bf16),
            jax.ShapeDtypeStruct((8, d_model), f32),
        ],
        in_specs=[pl.BlockSpec(memory_space=pltpu.SMEM)] + [pl.BlockSpec(memory_space=pl.ANY)] * 8,
        out_specs=[vmem] * 2,
        scratch_shapes=[
            pltpu.VMEM(latents.shape[1:], bf16),
            pltpu.VMEM((*up_qkv.shape[:2], cols // PLANE), bf16),
            *[pltpu.VMEM(array.shape, array.dtype) for array in operands[3:]],
            dma((8,)),
            pltpu.VMEM((2, rows, d_model), f32),
            pltpu.VMEM((tokens, d_model), bf16),
            pltpu.VMEM((2, n_z, PLANE, tokens, half), bf16),
            pltpu.VMEM((3, PLANE, w_rows, cols // PLANE), bf16),
            pltpu.VMEM((PLANE, *operands[1].shape), bf16),
            pltpu.VMEM((3, PLANE, w_rows, cols // PLANE), f32),
            pltpu.VMEM((n_head, PLANE * w_rows, width), bf16),
            pltpu.VMEM((n_head, 3, PLANE * tokens, width), bf16),
            pltpu.VMEM((n_head, 3, PLANE * tokens, width), bf16),
            pltpu.VMEM((n_head, 2, PLANE * tokens, width), f32),
            pltpu.VMEM((n_head, PLANE, tokens, HEAD_DIM), bf16),
            pltpu.VMEM((n_z, tokens, cols), bf16),
            pltpu.VMEM((PLANE, w_rows, cols), bf16),
            pltpu.VMEM((2, n_z, rows, block), f32),
            pltpu.VMEM((n_z, rows, block), f32),
            pltpu.VMEM((n_z, padded, block), bf16),
            pltpu.VMEM((n_z, padded, block), bf16),
            dma((2,)),
            dma((2, n_z - 1)),
            dma((2, PLANE - 1)),
            dma((2, PLANE)),
            dma((2, n_head, PLANE - 1, 3)),
            dma((2, PLANE - 1)),
            dma((2, n_head, 2)),
            dma((2, n_head)),
            dma((2, 3, 2)),
            dma((2, n_head, PLANE - 1)),
            dma((2, n_head, n_z - 1)),
            dma((2,)),
            dma((2, n_z - 1)),
        ],
        compiler_params=pltpu.CompilerParams(
            collective_id=0, has_side_effects=True, vmem_limit_bytes=56 * 1024 * 1024
        ),
        cost_estimate=pl.CostEstimate(
            flops=2 * n_fsdp * tokens * w_rows * 4 * cols,
            bytes_accessed=8 * w_rows * cols,
            transcendentals=0,
        ),
    )(
        step,
        latents[0],
        *operands,
    )
    velocity = (factors[0:1] * block_out.astype(f32)).astype(bf16)
    next_rows = (
        latents[0].astype(f32)
        + factors[1:2] * velocity.astype(f32)
        + factors[2:3] * step_noise[0].astype(f32)
    )
    return (velocity[None], next_rows.astype(bf16)[None])


def gather_weights(
    latents,
    step_noise,
    base_qkv,
    down_qkv,
    up_query_key_value,
    base_out,
    down_out,
    up_out,
    modulation,
    timestep,
):
    step_index = timestep[0]
    mod_rows = lax.dynamic_index_in_dim(modulation, step_index, 0, keepdims=False)
    latent_f = latents[0].astype(jnp.float32)
    mean_square = jnp.mean(latent_f * latent_f, axis=-1, keepdims=True)
    normalized_rows = (
        latent_f * lax.rsqrt(mean_square + EPSILON) * (1.0 + mod_rows[1]) + mod_rows[0]
    ).astype(jnp.bfloat16)
    head_cols = base_qkv.shape[2]
    seq_len = normalized_rows.shape[0] * lax.axis_size("sp")
    every_token = lax.all_gather(normalized_rows, "sp", axis=0, tiled=True)
    lowrank = jnp.einsum(
        "prk,pkc->prc", down_qkv, up_query_key_value, preferred_element_type=jnp.float32
    )
    merged_qkv = (base_qkv.astype(jnp.float32) + lowrank).astype(jnp.bfloat16)
    projected = jnp.einsum(
        "lr,prc->plc",
        every_token,
        lax.all_gather(merged_qkv, "fsdp", axis=1, tiled=True),
        preferred_element_type=jnp.float32,
    ).astype(jnp.bfloat16)
    heads_here = head_cols // HEAD_DIM
    split_heads = projected.reshape(3, seq_len, heads_here, HEAD_DIM).transpose(2, 0, 1, 3)

    def one_head(triple):
        scores = jnp.dot(triple[0], triple[1].T, preferred_element_type=jnp.float32) * (
            1.0 / HEAD_DIM**0.5
        )
        attention_weights = jax.nn.softmax(scores, axis=-1).astype(jnp.bfloat16)
        return jnp.dot(attention_weights, triple[2], preferred_element_type=jnp.float32).astype(
            jnp.bfloat16
        )

    per_head = lax.map(one_head, split_heads)
    attention_result = per_head.transpose(1, 0, 2).reshape(seq_len, head_cols)
    merged_out = (
        base_out.astype(jnp.float32) + jnp.dot(down_out, up_out, preferred_element_type=jnp.float32)
    ).astype(jnp.bfloat16)
    full_out = lax.all_gather(merged_out, "fsdp", axis=1, tiled=True)
    block_out = lax.psum_scatter(
        jnp.dot(attention_result, full_out, preferred_element_type=jnp.float32).astype(
            jnp.bfloat16
        ),
        "sp",
        scatter_dimension=0,
        tiled=True,
    ).astype(jnp.float32)
    velocity = ((1.0 + mod_rows[2]) * block_out).astype(jnp.bfloat16)
    position = step_index.astype(jnp.float32)
    step_size = plan_sigma(position + 1.0) - plan_sigma(position)
    next_rows = (
        latent_f
        + step_size * velocity.astype(jnp.float32)
        + NOISE_LEVEL * jnp.sqrt(-step_size) * step_noise[0].astype(jnp.float32)
    )
    return (velocity[None], next_rows.astype(jnp.bfloat16)[None])


def solution(mesh):
    in_specs = (
        P("fsdp", "sp", None),
        P("fsdp", "sp", None),
        P(None, "fsdp", "sp"),
        P(None, "fsdp", None),
        P(None, None, "sp"),
        P("sp", "fsdp"),
        P("sp", None),
        P(None, "fsdp"),
        P(),
        P("fsdp"),
    )
    out_specs = (P("fsdp", "sp", None), P("fsdp", "sp", None))
    return jax.shard_map(
        per_device, mesh=mesh, in_specs=in_specs, out_specs=out_specs, check_vma=False
    )
```

```python
import functools

import jax
import jax.numpy as jnp
from jax import lax
from jax.experimental import pallas as pl
from jax.experimental.pallas import tpu as pltpu
from jax.sharding import PartitionSpec as P

HEAD_DIM = 128
NSTEP = 16


EPSILON = 1e-06
SHIFT_FACTOR = 5.0
NOISE_LEVEL = 0.7


def plan_sigma(position):
    ramp = 1.0 - position / NSTEP
    return SHIFT_FACTOR * ramp / (1.0 + (SHIFT_FACTOR - 1.0) * ramp)


PLANE = 4
MESH = pl.DeviceIdType.MESH


def plane_kernel(
    n_z,
    step_ref,
    latents_hbm,
    base_qkv_hbm,
    down_qkv_hbm,
    up_qkv_hbm,
    base_out_hbm,
    down_out_hbm,
    up_out_hbm,
    mod_hbm,
    result_ref,
    gate_ref,
    step_size_ref,
    noise_size_ref,
    latents_ref,
    base_qkv_ref,
    down_qkv_ref,
    up_qkv_ref,
    base_out_ref,
    down_out_ref,
    up_out_ref,
    mod_ref,
    in_sem,
    latf,
    normed,
    acts,
    w_send,
    w_recv,
    part_send,
    part_recv,
    part_own,
    att_send,
    att_all,
    wo_all,
    out_half,
    out_sib,
    vel_send,
    vel_recv,
    lat_sem,
    x1_sem,
    x3_sem,
    xs_sem,
    w_sem,
    pair_sem,
    far_sem,
    wo_sem,
    at_sem,
    ag_sem,
    os_sem,
    v_sem,
):
    loads = {}
    for k, (source, target) in enumerate(
        (
            (latents_hbm, latents_ref),
            (base_qkv_hbm, base_qkv_ref),
            (down_qkv_hbm, down_qkv_ref),
            (up_qkv_hbm, up_qkv_ref),
            (mod_hbm, mod_ref),
            (base_out_hbm, base_out_ref),
            (down_out_hbm, down_out_ref),
            (up_out_hbm, up_out_ref),
        )
    ):
        loads[k] = pltpu.make_async_copy(source, target, in_sem.at[k])
        loads[k].start()
    f, c = lax.axis_index("fsdp"), lax.axis_index("sp")
    z, j = f // PLANE, f % PLANE
    rows, d_model = latents_ref.shape
    tokens = 2 * rows
    n_head = w_send.shape[0]
    block = d_model // n_z
    half = block // 2
    w_rows = base_qkv_ref.shape[1]
    x_at, y_at = j % 2, j // 2
    z_lo, z_hi = z % 2, z // 2
    x_near, y_near = 2 * y_at + 1 - x_at, 2 * (1 - y_at) + x_at
    width = 3 * HEAD_DIM
    f32, bf16 = jnp.float32, jnp.bfloat16

    def in_plane(d):
        return (z * PLANE + (j + d) % PLANE, c)

    def in_column(d):
        return (((z + d) % n_z) * PLANE + j, c)

    sibling = (f, 1 - c)
    x_device, y_device = (z * PLANE + x_near, c), (z * PLANE + y_near, c)
    z_pair = ((2 * z_hi + 1 - z_lo) * PLANE + j, c)
    z_far = ((2 * (1 - z_hi) + z_lo) * PLANE + j, c)

    def send(src, dst, sems, where, device):
        copy = pltpu.make_async_remote_copy(
            src_ref=src,
            dst_ref=dst,
            send_sem=sems.at[(0, *where)],
            recv_sem=sems.at[(1, *where)],
            device_id=device,
            device_id_type=MESH,
        )
        copy.start()
        return copy

    barrier = pltpu.get_barrier_semaphore()
    partners = [sibling]
    partners += [in_plane(d) for d in range(1, PLANE)]
    partners += [in_column(d) for d in range(1, n_z)]
    for partner in partners:
        pl.semaphore_signal(barrier, inc=1, device_id=partner, device_id_type=MESH)

    loads[0].wait()
    latf[c] = latents_ref[...].astype(f32)

    def merge(h):
        for p in range(3):
            ats = [(g * n_head + h) * HEAD_DIM for g in range(PLANE)]
            lowrank = lax.dot_general(
                down_qkv_ref[p],
                jnp.concatenate([up_qkv_ref[p, :, at : at + HEAD_DIM] for at in ats], axis=1),
                (((0,), (0,)), ((), ())),
                preferred_element_type=f32,
            )
            for g, at in enumerate(ats):
                w_send[h, g, :, p * HEAD_DIM : (p + 1) * HEAD_DIM] = (
                    base_qkv_ref[p, :, at : at + HEAD_DIM].astype(f32)
                    + lowrank[:, g * HEAD_DIM : (g + 1) * HEAD_DIM]
                ).astype(bf16)
        w_recv[h, j] = w_send[h, j]

    pl.semaphore_wait(barrier, len(partners))
    lat_copy = send(latf.at[c], latf.at[c], lat_sem, (), sibling)
    w_copies = {}

    def send_weights(h):
        for d in range(1, PLANE):
            w_copies[h, d] = send(
                w_send.at[h, (j + d) % PLANE], w_recv.at[h, j], w_sem, (h, d - 1), in_plane(d)
            )

    for k in (1, 2, 3):
        loads[k].wait()
    merge(0)
    send_weights(0)

    step_index = step_ref[0]
    loads[4].wait()

    def mod_row(k):
        return mod_ref[k, pl.ds(step_index, 1), :]

    lat_copy.wait_recv()
    lat_rows = latf[...].reshape(tokens, d_model)
    mean_square = jnp.mean(lat_rows * lat_rows, axis=-1, keepdims=True)
    normed[...] = (
        lat_rows * lax.rsqrt(mean_square + EPSILON) * (1.0 + mod_row(1)) + mod_row(0)
    ).astype(bf16)

    def features(z_at):
        return pl.ds(pl.multiple_of(z_at * block + c * half, half), half)

    own_half = pl.ds(pl.multiple_of(c * half, HEAD_DIM), half)
    x1 = [
        send(
            normed.at[:, features((z + d) % n_z)],
            acts.at[z, j, :, own_half],
            x1_sem,
            (d - 1,),
            in_column(d),
        )
        for d in range(1, n_z)
    ]
    acts[z, j, :, own_half] = normed[:, features(z)]
    if n_head > 1:
        merge(1)
    for copy in x1:
        copy.wait_recv()
    x3 = [
        send(acts.at[:, j, :, own_half], acts.at[:, j, :, own_half], x3_sem, (d - 1,), in_plane(d))
        for d in range(1, PLANE)
    ]
    xs = [send(acts.at[:, j, :, own_half], acts.at[:, j, :, own_half], xs_sem, (0,), sibling)]
    for h in range(2, n_head):
        merge(h)
    gate_ref[...] = 1.0 + mod_row(2)
    position = jnp.full((1, d_model), step_index.astype(f32), f32)
    step_size = plan_sigma(position + 1.0) - plan_sigma(position)
    step_size_ref[...] = step_size
    noise_size_ref[...] = NOISE_LEVEL * jnp.sqrt(-step_size)
    for k in (5, 6, 7):
        loads[k].wait()
    merged_out = (
        base_out_ref[...].astype(f32)
        + lax.dot_general(
            up_out_ref[...],
            down_out_ref[...],
            (((0,), (0,)), ((), ())),
            preferred_element_type=f32,
        )
    ).astype(bf16)
    for g in range(PLANE):
        for h in range(n_head):
            at, to = (g * n_head + h) * HEAD_DIM, (h * PLANE + g) * HEAD_DIM
            wo_all[j, :, to : to + HEAD_DIM] = merged_out[:, at : at + HEAD_DIM]
    for d in range(1, PLANE):
        x3[d - 1].wait_recv()
        came = (j + PLANE - d) % PLANE
        xs.append(send(acts.at[:, came, :, own_half], acts.at[:, came, :, own_half], xs_sem, (d,), sibling))
    if n_head > 1:
        send_weights(1)
    for copy in xs:
        copy.wait_recv()

    wo_x, wo_y, wo_far = [], [], []
    wo_half = w_rows // 2

    def send_out_rows(owner, k, where, device):
        view = wo_all.at[owner, pl.ds(k * wo_half, wo_half)]
        return send(view, view, wo_sem, where, device)

    pair_copies, far_copies = {}, {}
    def partial_sums(h):
        for d in range(1, PLANE):
            w_copies[h, d].wait_recv()
        if h == n_head - 1:
            for k in range(2):
                wo_x.append(send_out_rows(j, k, (0, k), x_device))
                wo_y.append(send_out_rows(j, 1 - k, (1, 1 - k), y_device))
        weights = w_recv[h].reshape(PLANE * w_rows, width)
        for parity in (1, 0):
            z_row = (z_lo + parity) % 2
            part = jnp.dot(
                jnp.concatenate(
                    [
                        acts[2 * ((z_hi + hi) % 2) + z_row].reshape(PLANE * tokens, block)
                        for hi in (1, 0)
                    ],
                    axis=0,
                ),
                weights,
                preferred_element_type=f32,
            )
            for hi in (1, 0):
                rows_hi = part[(1 - hi) * PLANE * tokens : (2 - hi) * PLANE * tokens]
                if parity:
                    part_send[h, hi] = rows_hi.astype(bf16)
                    pair_copies[h, hi] = send(
                        part_send.at[h, hi], part_recv.at[h, hi], pair_sem, (h, hi), z_pair
                    )
                else:
                    part_own[h, hi] = rows_hi

    def send_far(h):
        pair_copies[h, 1].wait_recv()
        part_send[h, 2] = (part_own[h, 1] + part_recv[h, 1].astype(f32)).astype(bf16)
        far_copies[h] = send(part_send.at[h, 2], part_recv.at[h, 2], far_sem, (h,), z_far)

    at_copies, ag_copies = {}, {}

    def lanes(h, g):
        return pl.ds(pl.multiple_of((h * PLANE + g) * HEAD_DIM, HEAD_DIM), HEAD_DIM)

    def spread(h):
        for d in range(1, PLANE):
            at_copies[h, d].wait_recv()
        chunk = pl.ds(h * PLANE * HEAD_DIM, PLANE * HEAD_DIM)
        for d in range(1, n_z):
            ag_copies[h, d] = send(
                att_all.at[z, :, chunk],
                att_all.at[z, :, chunk],
                ag_sem,
                (h, d - 1),
                in_column(d),
            )

    def attend(h):
        pair_copies[h, 0].wait_recv()
        far_copies[h].wait_recv()
        projected = (
            part_own[h, 0] + part_recv[h, 0].astype(f32) + part_recv[h, 2].astype(f32)
        ).astype(bf16)
        for s in range(PLANE):
            rows_s = projected[s * tokens : (s + 1) * tokens]
            query = rows_s[:, :HEAD_DIM]
            key = rows_s[:, HEAD_DIM : 2 * HEAD_DIM]
            value = rows_s[:, 2 * HEAD_DIM :]
            scores = lax.dot_general(
                query, key, (((1,), (1,)), ((), ())), preferred_element_type=f32
            ) * (1.0 / HEAD_DIM**0.5)
            weights = jnp.exp(scores - jnp.max(scores, axis=-1, keepdims=True))
            weights = weights / jnp.sum(weights, axis=-1, keepdims=True)
            att_send[h, s] = jnp.dot(
                weights.astype(bf16), value, preferred_element_type=f32
            ).astype(bf16)
        for d in range(1, PLANE):
            at_copies[h, d] = send(
                att_send.at[h, (j + d) % PLANE],
                att_all.at[z, :, lanes(h, j)],
                at_sem,
                (h, d - 1),
                in_plane(d),
            )
        att_all[z, :, lanes(h, j)] = att_send[h, j]

    for h in range(n_head):
        partial_sums(h)
        if h + 2 < n_head:
            send_weights(h + 2)
        if h:
            send_far(h - 1)
        if h > 1:
            attend(h - 2)
    send_far(n_head - 1)
    for h in range(max(n_head - 2, 0), n_head):
        if h:
            spread(h - 1)
        attend(h)
    wo_x[0].wait_recv()
    wo_far.append(send_out_rows(x_near, 0, (2, 0), y_device))
    wo_y[0].wait_recv()
    wo_far.append(send_out_rows(y_near, 1, (2, 1), x_device))
    spread(n_head - 1)

    for copy in (wo_x[1], wo_y[1], *wo_far):
        copy.wait_recv()
    out = None
    for h in range(n_head):
        for d in range(1, n_z):
            ag_copies[h, d].wait_recv()
        chunk = slice(h * PLANE * HEAD_DIM, (h + 1) * PLANE * HEAD_DIM)
        term = lax.dot_general(
            att_all[:, :, chunk].reshape(n_z * tokens, PLANE * HEAD_DIM),
            wo_all[:, :, chunk].reshape(block, PLANE * HEAD_DIM),
            (((1,), (1,)), ((), ())),
            preferred_element_type=f32,
        )
        out = term if out is None else out + term
    for s in range(n_z):
        for k in range(2):
            at = s * tokens + k * rows
            out_half[k, s] = out[at : at + rows]
    order = list(range(1, n_z)) + [0]
    os_copies = []
    for d in order:
        z_at = (z + d) % n_z
        os_copies.append(
            send(out_half.at[1 - c, z_at], out_sib.at[z_at], os_sem, (d,), sibling)
        )
    pad = jnp.zeros((vel_send.shape[1] - rows, block), f32)
    v_copies = []
    for k, d in enumerate(order):
        z_at = (z + d) % n_z
        os_copies[k].wait_recv()
        block_sum = out_half[c, z_at] + out_sib[z_at]
        block_sum = jnp.concatenate([block_sum, pad], axis=0).astype(bf16)
        if d:
            vel_send[z_at] = block_sum
            v_copies.append(
                send(vel_send.at[z_at], vel_recv.at[z], v_sem, (d - 1,), in_column(d))
            )
        else:
            vel_recv[z] = block_sum
    for copy in v_copies:
        copy.wait_recv()
    for s in range(n_z):
        result_ref[:, s * block : (s + 1) * block] = vel_recv[s, :rows]

    every = [lat_copy, *os_copies, *x1, *x3, *xs, *wo_x, *wo_y, *wo_far, *v_copies]
    for group in (w_copies, pair_copies, far_copies, at_copies, ag_copies):
        every += list(group.values())
    for copy in every:
        copy.wait_send()


def per_device(*args):
    latents, step_noise, base_qkv, down_qkv, up_qkv, base_out, down_out, up_out, modulation, step = (
        args
    )
    n_fsdp, n_sp = lax.axis_size("fsdp"), lax.axis_size("sp")
    _, rows, d_model = latents.shape
    heads_here = base_qkv.shape[2] // HEAD_DIM
    tokens = rows * n_sp
    if n_sp != 2 or n_fsdp != 4 * PLANE or heads_here % PLANE or tokens % 16:
        return gather_weights(*args)
    n_z, n_head = n_fsdp // PLANE, heads_here // PLANE
    block = d_model // n_z
    half = block // 2
    w_rows = base_qkv.shape[1]
    width = 3 * HEAD_DIM
    cols = base_qkv.shape[2]
    f32, bf16 = jnp.float32, jnp.bfloat16
    if half % HEAD_DIM or w_rows % 32 or block != PLANE * w_rows or base_out.shape[1] != w_rows:
        return gather_weights(*args)
    operands = (
        base_qkv,
        down_qkv.swapaxes(1, 2),
        up_qkv,
        base_out.T,
        down_out.T,
        up_out,
        modulation.swapaxes(0, 1),
    )
    padded = -(-rows // 16) * 16
    dma = pltpu.SemaphoreType.DMA
    vmem = pl.BlockSpec(memory_space=pltpu.VMEM)
    block_out, gate, step_size, noise_size = pl.pallas_call(
        functools.partial(plane_kernel, n_z),
        out_shape=[jax.ShapeDtypeStruct((rows, d_model), bf16)]
        + [jax.ShapeDtypeStruct((1, d_model), f32)] * 3,
        in_specs=[pl.BlockSpec(memory_space=pltpu.SMEM)] + [pl.BlockSpec(memory_space=pl.ANY)] * 8,
        out_specs=[vmem] * 4,
        scratch_shapes=[
            pltpu.VMEM(latents.shape[1:], bf16),
            *[pltpu.VMEM(array.shape, array.dtype) for array in operands],
            dma((8,)),
            pltpu.VMEM((2, rows, d_model), f32),
            pltpu.VMEM((tokens, d_model), bf16),
            pltpu.VMEM((n_z, PLANE, tokens, block), bf16),
            pltpu.VMEM((n_head, PLANE, w_rows, width), bf16),
            pltpu.VMEM((n_head, PLANE, w_rows, width), bf16),
            pltpu.VMEM((n_head, 3, PLANE * tokens, width), bf16),
            pltpu.VMEM((n_head, 3, PLANE * tokens, width), bf16),
            pltpu.VMEM((n_head, 2, PLANE * tokens, width), f32),
            pltpu.VMEM((n_head, PLANE, tokens, HEAD_DIM), bf16),
            pltpu.VMEM((n_z, tokens, cols), bf16),
            pltpu.VMEM((PLANE, w_rows, cols), bf16),
            pltpu.VMEM((2, n_z, rows, block), f32),
            pltpu.VMEM((n_z, rows, block), f32),
            pltpu.VMEM((n_z, padded, block), bf16),
            pltpu.VMEM((n_z, padded, block), bf16),
            dma((2,)),
            dma((2, n_z - 1)),
            dma((2, PLANE - 1)),
            dma((2, PLANE)),
            dma((2, n_head, PLANE - 1)),
            dma((2, n_head, 2)),
            dma((2, n_head)),
            dma((2, 3, 2)),
            dma((2, n_head, PLANE - 1)),
            dma((2, n_head, n_z - 1)),
            dma((2, n_z)),
            dma((2, n_z - 1)),
        ],
        compiler_params=pltpu.CompilerParams(
            collective_id=0, has_side_effects=True, vmem_limit_bytes=56 * 1024 * 1024
        ),
        cost_estimate=pl.CostEstimate(
            flops=2 * n_fsdp * tokens * w_rows * 4 * cols,
            bytes_accessed=8 * w_rows * cols,
            transcendentals=0,
        ),
    )(
        step,
        latents[0],
        *operands,
    )
    velocity = (gate * block_out.astype(f32)).astype(bf16)
    next_rows = (
        latents[0].astype(f32)
        + step_size * velocity.astype(f32)
        + noise_size * step_noise[0].astype(f32)
    )
    return (velocity[None], next_rows.astype(bf16)[None])


def gather_weights(
    latents,
    step_noise,
    base_qkv,
    down_qkv,
    up_query_key_value,
    base_out,
    down_out,
    up_out,
    modulation,
    timestep,
):
    step_index = timestep[0]
    mod_rows = lax.dynamic_index_in_dim(modulation, step_index, 0, keepdims=False)
    latent_f = latents[0].astype(jnp.float32)
    mean_square = jnp.mean(latent_f * latent_f, axis=-1, keepdims=True)
    normalized_rows = (
        latent_f * lax.rsqrt(mean_square + EPSILON) * (1.0 + mod_rows[1]) + mod_rows[0]
    ).astype(jnp.bfloat16)
    head_cols = base_qkv.shape[2]
    seq_len = normalized_rows.shape[0] * lax.axis_size("sp")
    every_token = lax.all_gather(normalized_rows, "sp", axis=0, tiled=True)
    lowrank = jnp.einsum(
        "prk,pkc->prc", down_qkv, up_query_key_value, preferred_element_type=jnp.float32
    )
    merged_qkv = (base_qkv.astype(jnp.float32) + lowrank).astype(jnp.bfloat16)
    projected = jnp.einsum(
        "lr,prc->plc",
        every_token,
        lax.all_gather(merged_qkv, "fsdp", axis=1, tiled=True),
        preferred_element_type=jnp.float32,
    ).astype(jnp.bfloat16)
    heads_here = head_cols // HEAD_DIM
    split_heads = projected.reshape(3, seq_len, heads_here, HEAD_DIM).transpose(2, 0, 1, 3)

    def one_head(triple):
        scores = jnp.dot(triple[0], triple[1].T, preferred_element_type=jnp.float32) * (
            1.0 / HEAD_DIM**0.5
        )
        attention_weights = jax.nn.softmax(scores, axis=-1).astype(jnp.bfloat16)
        return jnp.dot(attention_weights, triple[2], preferred_element_type=jnp.float32).astype(
            jnp.bfloat16
        )

    per_head = lax.map(one_head, split_heads)
    attention_result = per_head.transpose(1, 0, 2).reshape(seq_len, head_cols)
    merged_out = (
        base_out.astype(jnp.float32) + jnp.dot(down_out, up_out, preferred_element_type=jnp.float32)
    ).astype(jnp.bfloat16)
    full_out = lax.all_gather(merged_out, "fsdp", axis=1, tiled=True)
    block_out = lax.psum_scatter(
        jnp.dot(attention_result, full_out, preferred_element_type=jnp.float32).astype(
            jnp.bfloat16
        ),
        "sp",
        scatter_dimension=0,
        tiled=True,
    ).astype(jnp.float32)
    velocity = ((1.0 + mod_rows[2]) * block_out).astype(jnp.bfloat16)
    position = step_index.astype(jnp.float32)
    step_size = plan_sigma(position + 1.0) - plan_sigma(position)
    next_rows = (
        latent_f
        + step_size * velocity.astype(jnp.float32)
        + NOISE_LEVEL * jnp.sqrt(-step_size) * step_noise[0].astype(jnp.float32)
    )
    return (velocity[None], next_rows.astype(jnp.bfloat16)[None])


def solution(mesh):
    in_specs = (
        P("fsdp", "sp", None),
        P("fsdp", "sp", None),
        P(None, "fsdp", "sp"),
        P(None, "fsdp", None),
        P(None, None, "sp"),
        P("sp", "fsdp"),
        P("sp", None),
        P(None, "fsdp"),
        P(),
        P("fsdp"),
    )
    out_specs = (P("fsdp", "sp", None), P("fsdp", "sp", None))
    return jax.shard_map(
        per_device, mesh=mesh, in_specs=in_specs, out_specs=out_specs, check_vma=False
    )
```

```python
import functools

import jax
import jax.numpy as jnp
from jax import lax
from jax.experimental import pallas as pl
from jax.experimental.pallas import tpu as pltpu
from jax.sharding import PartitionSpec as P

HEAD_DIM = 128
NSTEP = 16


EPSILON = 1e-06
SHIFT_FACTOR = 5.0
NOISE_LEVEL = 0.7


def plan_sigma(position):
    ramp = 1.0 - position / NSTEP
    return SHIFT_FACTOR * ramp / (1.0 + (SHIFT_FACTOR - 1.0) * ramp)


PLANE = 4
MESH = pl.DeviceIdType.MESH


def plane_kernel(
    n_z,
    step_ref,
    latents_hbm,
    base_qkv_hbm,
    down_qkv_hbm,
    up_qkv_hbm,
    base_out_hbm,
    down_out_hbm,
    up_out_hbm,
    mod_hbm,
    result_ref,
    gate_ref,
    step_size_ref,
    noise_size_ref,
    latents_ref,
    base_qkv_ref,
    down_qkv_ref,
    up_qkv_ref,
    base_out_ref,
    down_out_ref,
    up_out_ref,
    mod_ref,
    in_sem,
    latf,
    normed,
    acts,
    w_send,
    w_recv,
    part_send,
    part_recv,
    part_own,
    att_send,
    att_all,
    wo_all,
    out_half,
    out_sib,
    vel_send,
    vel_recv,
    lat_sem,
    x1_sem,
    x3_sem,
    xs_sem,
    w_sem,
    pair_sem,
    far_sem,
    wo_sem,
    at_sem,
    ag_sem,
    os_sem,
    v_sem,
):
    loads = {}
    for k, (source, target) in enumerate(
        (
            (latents_hbm, latents_ref),
            (base_qkv_hbm, base_qkv_ref),
            (down_qkv_hbm, down_qkv_ref),
            (up_qkv_hbm, up_qkv_ref),
            (mod_hbm, mod_ref),
            (base_out_hbm, base_out_ref),
            (down_out_hbm, down_out_ref),
            (up_out_hbm, up_out_ref),
        )
    ):
        loads[k] = pltpu.make_async_copy(source, target, in_sem.at[k])
        loads[k].start()
    f, c = lax.axis_index("fsdp"), lax.axis_index("sp")
    z, j = f // PLANE, f % PLANE
    rows, d_model = latents_ref.shape
    tokens = 2 * rows
    n_head = w_send.shape[0]
    block = d_model // n_z
    half = block // 2
    w_rows = base_qkv_ref.shape[1]
    x_at, y_at = j % 2, j // 2
    z_lo, z_hi = z % 2, z // 2
    x_near, y_near = 2 * y_at + 1 - x_at, 2 * (1 - y_at) + x_at
    width = 3 * HEAD_DIM
    f32, bf16 = jnp.float32, jnp.bfloat16

    def in_plane(d):
        return (z * PLANE + (j + d) % PLANE, c)

    def in_column(d):
        return (((z + d) % n_z) * PLANE + j, c)

    sibling = (f, 1 - c)
    x_device, y_device = (z * PLANE + x_near, c), (z * PLANE + y_near, c)
    z_pair = ((2 * z_hi + 1 - z_lo) * PLANE + j, c)
    z_far = ((2 * (1 - z_hi) + z_lo) * PLANE + j, c)

    def send(src, dst, sems, where, device):
        copy = pltpu.make_async_remote_copy(
            src_ref=src,
            dst_ref=dst,
            send_sem=sems.at[(0, *where)],
            recv_sem=sems.at[(1, *where)],
            device_id=device,
            device_id_type=MESH,
        )
        copy.start()
        return copy

    barrier = pltpu.get_barrier_semaphore()
    partners = [sibling]
    partners += [in_plane(d) for d in range(1, PLANE)]
    partners += [in_column(d) for d in range(1, n_z)]
    for partner in partners:
        pl.semaphore_signal(barrier, inc=1, device_id=partner, device_id_type=MESH)

    loads[0].wait()
    latf[c] = latents_ref[...].astype(f32)

    def merge(h):
        for p in range(3):
            ats = [(g * n_head + h) * HEAD_DIM for g in range(PLANE)]
            lowrank = lax.dot_general(
                down_qkv_ref[p],
                jnp.concatenate([up_qkv_ref[p, :, at : at + HEAD_DIM] for at in ats], axis=1),
                (((0,), (0,)), ((), ())),
                preferred_element_type=f32,
            )
            for g, at in enumerate(ats):
                w_send[h, g, :, p * HEAD_DIM : (p + 1) * HEAD_DIM] = (
                    base_qkv_ref[p, :, at : at + HEAD_DIM].astype(f32)
                    + lowrank[:, g * HEAD_DIM : (g + 1) * HEAD_DIM]
                ).astype(bf16)
        w_recv[h, j] = w_send[h, j]

    pl.semaphore_wait(barrier, len(partners))
    lat_copy = send(latf.at[c], latf.at[c], lat_sem, (), sibling)
    w_copies = {}

    def send_weights(h):
        for d in range(1, PLANE):
            w_copies[h, d] = send(
                w_send.at[h, (j + d) % PLANE], w_recv.at[h, j], w_sem, (h, d - 1), in_plane(d)
            )

    for k in (1, 2, 3):
        loads[k].wait()
    merge(0)
    send_weights(0)

    step_index = step_ref[0]
    loads[4].wait()

    def mod_row(k):
        return mod_ref[k, pl.ds(step_index, 1), :]

    lat_copy.wait_recv()
    lat_rows = latf[...].reshape(tokens, d_model)
    mean_square = jnp.mean(lat_rows * lat_rows, axis=-1, keepdims=True)
    normed[...] = (
        lat_rows * lax.rsqrt(mean_square + EPSILON) * (1.0 + mod_row(1)) + mod_row(0)
    ).astype(bf16)

    def features(z_at):
        return pl.ds(pl.multiple_of(z_at * block + c * half, half), half)

    own_half = pl.ds(pl.multiple_of(c * half, HEAD_DIM), half)
    x1 = [
        send(
            normed.at[:, features((z + d) % n_z)],
            acts.at[z, j, :, own_half],
            x1_sem,
            (d - 1,),
            in_column(d),
        )
        for d in range(1, n_z)
    ]
    acts[z, j, :, own_half] = normed[:, features(z)]
    if n_head > 1:
        merge(1)
    for copy in x1:
        copy.wait_recv()
    x3 = [
        send(acts.at[:, j, :, own_half], acts.at[:, j, :, own_half], x3_sem, (d - 1,), in_plane(d))
        for d in range(1, PLANE)
    ]
    xs = [send(acts.at[:, j, :, own_half], acts.at[:, j, :, own_half], xs_sem, (0,), sibling)]
    for h in range(2, n_head):
        merge(h)
    gate_ref[...] = 1.0 + mod_row(2)
    position = jnp.full((1, d_model), step_index.astype(f32), f32)
    step_size = plan_sigma(position + 1.0) - plan_sigma(position)
    step_size_ref[...] = step_size
    noise_size_ref[...] = NOISE_LEVEL * jnp.sqrt(-step_size)
    for k in (5, 6, 7):
        loads[k].wait()
    merged_out = (
        base_out_ref[...].astype(f32)
        + lax.dot_general(
            up_out_ref[...],
            down_out_ref[...],
            (((0,), (0,)), ((), ())),
            preferred_element_type=f32,
        )
    ).astype(bf16)
    for g in range(PLANE):
        for h in range(n_head):
            at, to = (g * n_head + h) * HEAD_DIM, (h * PLANE + g) * HEAD_DIM
            wo_all[j, :, to : to + HEAD_DIM] = merged_out[:, at : at + HEAD_DIM]
    for d in range(1, PLANE):
        x3[d - 1].wait_recv()
        came = (j + PLANE - d) % PLANE
        xs.append(send(acts.at[:, came, :, own_half], acts.at[:, came, :, own_half], xs_sem, (d,), sibling))
    if n_head > 1:
        send_weights(1)
    for copy in xs:
        copy.wait_recv()

    wo_x, wo_y, wo_far = [], [], []
    wo_half = w_rows // 2

    def send_out_rows(owner, k, where, device):
        view = wo_all.at[owner, pl.ds(k * wo_half, wo_half)]
        return send(view, view, wo_sem, where, device)

    pair_copies, far_copies = {}, {}

    def send_pair(h, hi):
        pair_copies[h, hi] = send(
            part_send.at[h, hi], part_recv.at[h, hi], pair_sem, (h, hi), z_pair
        )

    def partial_sums(h):
        for d in range(1, PLANE):
            w_copies[h, d].wait_recv()
        if h == n_head - 1:
            for k in range(2):
                wo_x.append(send_out_rows(j, k, (0, k), x_device))
                wo_y.append(send_out_rows(j, 1 - k, (1, 1 - k), y_device))
        weights = w_recv[h].reshape(PLANE * w_rows, width)
        for parity in (1, 0):
            z_row = (z_lo + parity) % 2
            part = jnp.dot(
                jnp.concatenate(
                    [
                        acts[2 * ((z_hi + hi) % 2) + z_row].reshape(PLANE * tokens, block)
                        for hi in (1, 0)
                    ],
                    axis=0,
                ),
                weights,
                preferred_element_type=f32,
            )
            for hi in (1, 0):
                rows_hi = part[(1 - hi) * PLANE * tokens : (2 - hi) * PLANE * tokens]
                if parity:
                    part_send[h, hi] = rows_hi.astype(bf16)
                    if hi or h < n_head - 1:
                        send_pair(h, hi)
                else:
                    part_own[h, hi] = rows_hi

    def send_far(h):
        pair_copies[h, 1].wait_recv()
        part_send[h, 2] = (part_own[h, 1] + part_recv[h, 1].astype(f32)).astype(bf16)
        far_copies[h] = send(part_send.at[h, 2], part_recv.at[h, 2], far_sem, (h,), z_far)
        if h == n_head - 1:
            send_pair(h, 0)

    at_copies, ag_copies = {}, {}

    def lanes(h, g):
        return pl.ds(pl.multiple_of((h * PLANE + g) * HEAD_DIM, HEAD_DIM), HEAD_DIM)

    def spread(h):
        for d in range(1, PLANE):
            at_copies[h, d].wait_recv()
        chunk = pl.ds(h * PLANE * HEAD_DIM, PLANE * HEAD_DIM)
        for d in range(1, n_z):
            ag_copies[h, d] = send(
                att_all.at[z, :, chunk],
                att_all.at[z, :, chunk],
                ag_sem,
                (h, d - 1),
                in_column(d),
            )

    def attend(h):
        pair_copies[h, 0].wait_recv()
        far_copies[h].wait_recv()
        projected = (
            part_own[h, 0] + part_recv[h, 0].astype(f32) + part_recv[h, 2].astype(f32)
        ).astype(bf16)
        for s in range(PLANE):
            rows_s = projected[s * tokens : (s + 1) * tokens]
            query = rows_s[:, :HEAD_DIM]
            key = rows_s[:, HEAD_DIM : 2 * HEAD_DIM]
            value = rows_s[:, 2 * HEAD_DIM :]
            scores = lax.dot_general(
                query, key, (((1,), (1,)), ((), ())), preferred_element_type=f32
            ) * (1.0 / HEAD_DIM**0.5)
            weights = jnp.exp(scores - jnp.max(scores, axis=-1, keepdims=True))
            weights = weights / jnp.sum(weights, axis=-1, keepdims=True)
            att_send[h, s] = jnp.dot(
                weights.astype(bf16), value, preferred_element_type=f32
            ).astype(bf16)
        for d in range(1, PLANE):
            at_copies[h, d] = send(
                att_send.at[h, (j + d) % PLANE],
                att_all.at[z, :, lanes(h, j)],
                at_sem,
                (h, d - 1),
                in_plane(d),
            )
        att_all[z, :, lanes(h, j)] = att_send[h, j]

    for h in range(n_head):
        partial_sums(h)
        if h + 2 < n_head:
            send_weights(h + 2)
        if h:
            send_far(h - 1)
        if h > 1:
            attend(h - 2)
    send_far(n_head - 1)
    for h in range(max(n_head - 2, 0), n_head):
        if h:
            spread(h - 1)
        attend(h)
    wo_x[0].wait_recv()
    wo_far.append(send_out_rows(x_near, 0, (2, 0), y_device))
    wo_y[0].wait_recv()
    wo_far.append(send_out_rows(y_near, 1, (2, 1), x_device))
    spread(n_head - 1)

    for copy in (wo_x[1], wo_y[1], *wo_far):
        copy.wait_recv()
    out = None
    for h in range(n_head):
        for d in range(1, n_z):
            ag_copies[h, d].wait_recv()
        chunk = slice(h * PLANE * HEAD_DIM, (h + 1) * PLANE * HEAD_DIM)
        term = lax.dot_general(
            att_all[:, :, chunk].reshape(n_z * tokens, PLANE * HEAD_DIM),
            wo_all[:, :, chunk].reshape(block, PLANE * HEAD_DIM),
            (((1,), (1,)), ((), ())),
            preferred_element_type=f32,
        )
        out = term if out is None else out + term
    for s in range(n_z):
        for k in range(2):
            at = s * tokens + k * rows
            out_half[k, s] = out[at : at + rows]
    order = list(range(1, n_z)) + [0]
    os_copies = []
    for d in order:
        z_at = (z + d) % n_z
        os_copies.append(
            send(out_half.at[1 - c, z_at], out_sib.at[z_at], os_sem, (d,), sibling)
        )
    pad = jnp.zeros((vel_send.shape[1] - rows, block), f32)
    v_copies = []
    for k, d in enumerate(order):
        z_at = (z + d) % n_z
        os_copies[k].wait_recv()
        block_sum = out_half[c, z_at] + out_sib[z_at]
        block_sum = jnp.concatenate([block_sum, pad], axis=0).astype(bf16)
        if d:
            vel_send[z_at] = block_sum
            v_copies.append(
                send(vel_send.at[z_at], vel_recv.at[z], v_sem, (d - 1,), in_column(d))
            )
        else:
            vel_recv[z] = block_sum
    for copy in v_copies:
        copy.wait_recv()
    for s in range(n_z):
        result_ref[:, s * block : (s + 1) * block] = vel_recv[s, :rows]

    every = [lat_copy, *os_copies, *x1, *x3, *xs, *wo_x, *wo_y, *wo_far, *v_copies]
    for group in (w_copies, pair_copies, far_copies, at_copies, ag_copies):
        every += list(group.values())
    for copy in every:
        copy.wait_send()


def per_device(*args):
    latents, step_noise, base_qkv, down_qkv, up_qkv, base_out, down_out, up_out, modulation, step = (
        args
    )
    n_fsdp, n_sp = lax.axis_size("fsdp"), lax.axis_size("sp")
    _, rows, d_model = latents.shape
    heads_here = base_qkv.shape[2] // HEAD_DIM
    tokens = rows * n_sp
    if n_sp != 2 or n_fsdp != 4 * PLANE or heads_here % PLANE or tokens % 16:
        return gather_weights(*args)
    n_z, n_head = n_fsdp // PLANE, heads_here // PLANE
    block = d_model // n_z
    half = block // 2
    w_rows = base_qkv.shape[1]
    width = 3 * HEAD_DIM
    cols = base_qkv.shape[2]
    f32, bf16 = jnp.float32, jnp.bfloat16
    if half % HEAD_DIM or w_rows % 32 or block != PLANE * w_rows or base_out.shape[1] != w_rows:
        return gather_weights(*args)
    operands = (
        base_qkv,
        down_qkv.swapaxes(1, 2),
        up_qkv,
        base_out.T,
        down_out.T,
        up_out,
        modulation.swapaxes(0, 1),
    )
    padded = -(-rows // 16) * 16
    dma = pltpu.SemaphoreType.DMA
    vmem = pl.BlockSpec(memory_space=pltpu.VMEM)
    block_out, gate, step_size, noise_size = pl.pallas_call(
        functools.partial(plane_kernel, n_z),
        out_shape=[jax.ShapeDtypeStruct((rows, d_model), bf16)]
        + [jax.ShapeDtypeStruct((1, d_model), f32)] * 3,
        in_specs=[pl.BlockSpec(memory_space=pltpu.SMEM)] + [pl.BlockSpec(memory_space=pl.ANY)] * 8,
        out_specs=[vmem] * 4,
        scratch_shapes=[
            pltpu.VMEM(latents.shape[1:], bf16),
            *[pltpu.VMEM(array.shape, array.dtype) for array in operands],
            dma((8,)),
            pltpu.VMEM((2, rows, d_model), f32),
            pltpu.VMEM((tokens, d_model), bf16),
            pltpu.VMEM((n_z, PLANE, tokens, block), bf16),
            pltpu.VMEM((n_head, PLANE, w_rows, width), bf16),
            pltpu.VMEM((n_head, PLANE, w_rows, width), bf16),
            pltpu.VMEM((n_head, 3, PLANE * tokens, width), bf16),
            pltpu.VMEM((n_head, 3, PLANE * tokens, width), bf16),
            pltpu.VMEM((n_head, 2, PLANE * tokens, width), f32),
            pltpu.VMEM((n_head, PLANE, tokens, HEAD_DIM), bf16),
            pltpu.VMEM((n_z, tokens, cols), bf16),
            pltpu.VMEM((PLANE, w_rows, cols), bf16),
            pltpu.VMEM((2, n_z, rows, block), f32),
            pltpu.VMEM((n_z, rows, block), f32),
            pltpu.VMEM((n_z, padded, block), bf16),
            pltpu.VMEM((n_z, padded, block), bf16),
            dma((2,)),
            dma((2, n_z - 1)),
            dma((2, PLANE - 1)),
            dma((2, PLANE)),
            dma((2, n_head, PLANE - 1)),
            dma((2, n_head, 2)),
            dma((2, n_head)),
            dma((2, 3, 2)),
            dma((2, n_head, PLANE - 1)),
            dma((2, n_head, n_z - 1)),
            dma((2, n_z)),
            dma((2, n_z - 1)),
        ],
        compiler_params=pltpu.CompilerParams(
            collective_id=0, has_side_effects=True, vmem_limit_bytes=56 * 1024 * 1024
        ),
        cost_estimate=pl.CostEstimate(
            flops=2 * n_fsdp * tokens * w_rows * 4 * cols,
            bytes_accessed=8 * w_rows * cols,
            transcendentals=0,
        ),
    )(
        step,
        latents[0],
        *operands,
    )
    velocity = (gate * block_out.astype(f32)).astype(bf16)
    next_rows = (
        latents[0].astype(f32)
        + step_size * velocity.astype(f32)
        + noise_size * step_noise[0].astype(f32)
    )
    return (velocity[None], next_rows.astype(bf16)[None])


def gather_weights(
    latents,
    step_noise,
    base_qkv,
    down_qkv,
    up_query_key_value,
    base_out,
    down_out,
    up_out,
    modulation,
    timestep,
):
    step_index = timestep[0]
    mod_rows = lax.dynamic_index_in_dim(modulation, step_index, 0, keepdims=False)
    latent_f = latents[0].astype(jnp.float32)
    mean_square = jnp.mean(latent_f * latent_f, axis=-1, keepdims=True)
    normalized_rows = (
        latent_f * lax.rsqrt(mean_square + EPSILON) * (1.0 + mod_rows[1]) + mod_rows[0]
    ).astype(jnp.bfloat16)
    head_cols = base_qkv.shape[2]
    seq_len = normalized_rows.shape[0] * lax.axis_size("sp")
    every_token = lax.all_gather(normalized_rows, "sp", axis=0, tiled=True)
    lowrank = jnp.einsum(
        "prk,pkc->prc", down_qkv, up_query_key_value, preferred_element_type=jnp.float32
    )
    merged_qkv = (base_qkv.astype(jnp.float32) + lowrank).astype(jnp.bfloat16)
    projected = jnp.einsum(
        "lr,prc->plc",
        every_token,
        lax.all_gather(merged_qkv, "fsdp", axis=1, tiled=True),
        preferred_element_type=jnp.float32,
    ).astype(jnp.bfloat16)
    heads_here = head_cols // HEAD_DIM
    split_heads = projected.reshape(3, seq_len, heads_here, HEAD_DIM).transpose(2, 0, 1, 3)

    def one_head(triple):
        scores = jnp.dot(triple[0], triple[1].T, preferred_element_type=jnp.float32) * (
            1.0 / HEAD_DIM**0.5
        )
        attention_weights = jax.nn.softmax(scores, axis=-1).astype(jnp.bfloat16)
        return jnp.dot(attention_weights, triple[2], preferred_element_type=jnp.float32).astype(
            jnp.bfloat16
        )

    per_head = lax.map(one_head, split_heads)
    attention_result = per_head.transpose(1, 0, 2).reshape(seq_len, head_cols)
    merged_out = (
        base_out.astype(jnp.float32) + jnp.dot(down_out, up_out, preferred_element_type=jnp.float32)
    ).astype(jnp.bfloat16)
    full_out = lax.all_gather(merged_out, "fsdp", axis=1, tiled=True)
    block_out = lax.psum_scatter(
        jnp.dot(attention_result, full_out, preferred_element_type=jnp.float32).astype(
            jnp.bfloat16
        ),
        "sp",
        scatter_dimension=0,
        tiled=True,
    ).astype(jnp.float32)
    velocity = ((1.0 + mod_rows[2]) * block_out).astype(jnp.bfloat16)
    position = step_index.astype(jnp.float32)
    step_size = plan_sigma(position + 1.0) - plan_sigma(position)
    next_rows = (
        latent_f
        + step_size * velocity.astype(jnp.float32)
        + NOISE_LEVEL * jnp.sqrt(-step_size) * step_noise[0].astype(jnp.float32)
    )
    return (velocity[None], next_rows.astype(jnp.bfloat16)[None])


def solution(mesh):
    in_specs = (
        P("fsdp", "sp", None),
        P("fsdp", "sp", None),
        P(None, "fsdp", "sp"),
        P(None, "fsdp", None),
        P(None, None, "sp"),
        P("sp", "fsdp"),
        P("sp", None),
        P(None, "fsdp"),
        P(),
        P("fsdp"),
    )
    out_specs = (P("fsdp", "sp", None), P("fsdp", "sp", None))
    return jax.shard_map(
        per_device, mesh=mesh, in_specs=in_specs, out_specs=out_specs, check_vma=False
    )
```
